512 devices in a mesh: group: 16 (over x, y), dom: 32 (over z, core).
Axes of the slice: x: 4, y: 4, z: 16, core: 2. Of those that a mesh axis runs over, the one named last changes fastest.
Arguments:
- cell_dofs: float32 [9, 56, 131072], P(None, None, ('group', 'dom')), may hold values from -6 to 6
- star_matrix: float32 [3, 9, 9, 131072], P(None, None, None, ('group', 'dom')), may hold values from -1.8 to 1.8
- stiffness: float32 [3, 56, 56], replicated, may hold values from -0.75 to 0.75
- volume_kernel: float32 [3, 56, 56], replicated, may hold values from -0.75 to 0.75
- flux_local: float32 [4, 9, 9, 131072], P(None, None, None, ('group', 'dom')), may hold values from -0.9 to 0.9
- flux_neigh: float32 [4, 9, 9, 131072], P(None, None, None, ('group', 'dom')), may hold values from -0.9 to 0.9
- face_proj: float32 [4, 21, 56], replicated, may hold values from -0.75 to 0.75
- face_lift: float32 [4, 56, 21], replicated, may hold values from -1.25 to 1.25
- face_perm: float32 [3, 21, 21], replicated, may hold values from -1.25 to 1.25
- point_proj: float32 [4, 49, 56], replicated, may hold values from -0.75 to 0.75
- point_lift: float32 [4, 56, 49], replicated, may hold values from -0.875 to 0.875
- neighbour: int32 [4, 131072], P(None, ('group', 'dom')), may hold values from 0 to 351
- face_code: int32 [4, 131072], P(None, ('group', 'dom')), may hold values from 0 to 11
- send_near: int32 [2048, 16], P(('group', 'dom')), may hold values from 0 to 255
- send_strike: int32 [1024, 16], P(('group', 'dom')), may hold values from 0 to 255
- fault_minus: int32 [65536], P(('group', 'dom')), may hold values from 0 to 1023
- fault_send: int32 [2560, 32], P(('group', 'dom')), may hold values from 0 to 1023, as said below
- fault_plus: int32 [65536], P(('group', 'dom')), may hold values from 0 to 639, as said below
- fault_live: int32 [16, 32], P('group', 'dom'), may hold values from 1 to 128, 1536 in all within a row
- normal_load: float32 [65536], P(('group', 'dom')), may hold values from 1 to 8
- shear_load: float32 [65536], P(('group', 'dom')), may hold values from -4 to 4
- direct_effect: float32 [65536], P(('group', 'dom')), may hold values from 0.2 to 0.6
- state_var: float32 [65536], P(('group', 'dom')), may hold values from 0 to 1.5
Outputs:
- new_dofs: float32 [9, 56, 131072], P(None, None, ('group', 'dom'))
- slip_rate: float32 [6, 49, 65536], P(None, None, ('group', 'dom'))
The draws below stay inside these ranges and needn't reach their ends.
Inputs may be any that keep to these rules, and one draw needn't show every extreme that they name: `fault_send`: each entry is a cell times 4 plus its fault face; the last entry of every list is cell 256 - 1 through face 3. The face in fault_plus equals the face of the list entry that it names; a slot names only lists whose sending partition lies inside the group; the share of slots per offset differs from partition to partition, and offset 0 means a far side in the same partition. `fault_live`: slots below this count are live, the others are empty.
All inputs are finite; a program needn't handle non-finite values. No bound on the sum of `fault_live` on one device may be relied on, other than what follows from the above.
Results may differ from the reference program's by a relative error of at most 0.0003.
Values sent between devices are 32-bit elements; how exact they have to be, the bound alone decides.
A program may use at most 128 MiB of HBM per device.

```python
import math
import jax
import jax.numpy as jnp
import numpy as np
from jax import lax

Q = 9
B = 56
FB = 21
NP = 49
NT = 6
NDER = 6
NEWTON = 4
CELLS_DEV = 256
HALO = 16
GHALO = 16
FAULT_DEV = 128
FAULT_MEAN = 48
EXT = 352
CELLS = 131072
FAULTS = 65536
N_GROUP = 16
N_DOM = 32
DEVICES = 512


def fault_tables(key):
    device_total = N_GROUP * N_DOM
    peer_slots = FAULT_DEV // 4
    cell_key, face_key, weight_key, pick_key, entry_key = jax.random.split(key, 5)
    cell_ids = jax.random.randint(cell_key, (device_total, 5, peer_slots), 0, CELLS_DEV)
    face_ids = jax.random.randint(face_key, (device_total, 5, peer_slots), 0, 4)
    cell_ids = cell_ids.at[:, :, peer_slots - 1].set(CELLS_DEV - 1)
    face_ids = face_ids.at[:, :, peer_slots - 1].set(3)
    offset_table = jnp.array([-2, -1, 0, 1, 2], dtype=jnp.int32)
    owners = jnp.arange(device_total, dtype=jnp.int32)
    rank_id = owners % N_DOM
    group_id = owners // N_DOM
    source = rank_id[:, None] - offset_table[None, :]
    usable = ((source >= 0) & (source < N_DOM)).astype(jnp.int32)
    shares = jax.random.randint(weight_key, (device_total, 5), 1, 17) * usable
    bounds = jnp.cumsum(shares, axis=1)
    total = bounds[:, 4]
    drawn = jax.random.randint(pick_key, (device_total, FAULT_DEV), 0, 1 << 20) % total[:, None]
    list_id = jnp.sum((drawn[:, :, None] >= bounds[:, None, :]).astype(jnp.int32), axis=2)
    entry_id = jax.random.randint(entry_key, (device_total, FAULT_DEV), 0, peer_slots)
    last_list = jnp.where(rank_id >= 2, 4, 2).astype(jnp.int32)
    list_id = list_id.at[:, FAULT_DEV - 1].set(last_list)
    entry_id = entry_id.at[:, FAULT_DEV - 1].set(peer_slots - 1)
    sender = group_id[:, None] * N_DOM + rank_id[:, None] - jnp.take(offset_table, list_id)
    picked = face_ids[sender, list_id, entry_id]
    slot_codes = (list_id * peer_slots + entry_id) * 4 + picked
    return (cell_ids.astype(jnp.int32), face_ids.astype(jnp.int32), slot_codes.astype(jnp.int32))


def draw_fault_send(key, part):
    cell_ids, face_ids, slot_codes = fault_tables(key)
    codes = cell_ids * 4 + face_ids
    return codes.reshape(N_GROUP * N_DOM * 5, FAULT_DEV // 4).astype(jnp.int32)


def draw_fault_plus(key, part):
    cell_ids, face_ids, slot_codes = fault_tables(key)
    return slot_codes.reshape(N_GROUP * N_DOM * FAULT_DEV).astype(jnp.int32)


def set_ends(values, own_key, low, largest):
    dims = values.shape
    spot = [jax.random.randint(jax.random.fold_in(own_key, axis), (), 0, dims[axis]) for axis in range(len(dims))]
    values = values.at[tuple(spot)].set(low)
    longest = dims.index(max(dims))
    spot[longest] = (spot[longest] + 1) % dims[longest]
    return values.at[tuple(spot)].set(largest)


def block_scale(stream_key, extent, shards, smallest, top_value):
    level = 1.0
    for dim, shards_of in shards:
        heights = jax.random.uniform(jax.random.fold_in(jax.random.fold_in(stream_key, 6), dim), (shards_of,), jnp.float32, smallest / len(shards), top_value / len(shards))
        level = level * jnp.repeat(jnp.exp(heights), extent[dim] // shards_of).reshape((-1,) + (1,) * (len(extent) - 1 - dim))
    return level


def split_up(number_of, total, most, skew):
    weights = [(1 << 20) // math.isqrt(rank ** skew) + 1 for rank in range(2, number_of + 1)]
    spare, holding = total - most - (number_of - 1), [1] * (number_of - 1)
    while spare > 0:
        candidates = [i for i in range(number_of - 1) if holding[i] < most]
        whole, remaining = sum([weights[i] for i in candidates]), spare
        for i in candidates:
            extra = min(most - holding[i], max(1, remaining * weights[i] // whole), spare)
            holding[i] = holding[i] + extra
            spare = spare - extra
    return np.array([most] + holding)


def ragged(own_key, count, total, most, lean):
    if count == 2:
        one = jax.random.randint(own_key, (), max(1, total - most), min(most, total - 1) + 1)
        return jnp.stack([one, total - one])
    sizes = jnp.asarray(split_up(count, total, most, lean), jnp.int32)
    pairs = (count - 1) // 2
    source_of, taker = sizes[1:1 + 2 * pairs:2], sizes[2:2 + 2 * pairs:2]
    slack = jnp.minimum(source_of - 1, most - taker)
    shifted = jax.random.randint(jax.random.fold_in(own_key, 1), (pairs,), 0, 1 << 20) % (slack + 1)
    sizes = sizes.at[1:1 + 2 * pairs:2].set(source_of - shifted).at[2:2 + 2 * pairs:2].set(taker + shifted)
    return sizes[jax.random.permutation(jax.random.fold_in(own_key, 2), count)]


def noise(stream_key, dims, scale, most, cuts=(), held_as=jnp.bfloat16):
    values = jax.random.normal(stream_key, dims, jnp.float32) * scale
    if len(cuts) > 0:
        values = block_scale(stream_key, dims, cuts, -0.22, 0.18) * values
    return jnp.clip(values, min=-most, max=most).astype(held_as)


def setup_inputs(seed: int = 0) -> dict:
    streams_of = jax.random.split(jax.random.key(seed), 24)
    return {
        "cell_dofs": noise(streams_of[0], (Q, B, CELLS), 1.0, 6.0, ((2, 512),), jnp.float32),
        "star_matrix": noise(streams_of[1], (3, Q, Q, CELLS), 0.3, 1.8, ((3, 512),), jnp.float32),
        "stiffness": noise(streams_of[2], (3, B, B), B ** -0.5, 0.75, (), jnp.float32),
        "volume_kernel": noise(streams_of[3], (3, B, B), B ** -0.5, 0.75, (), jnp.float32),
        "flux_local": noise(streams_of[4], (4, Q, Q, CELLS), 0.15, 0.9, ((3, 512),), jnp.float32),
        "flux_neigh": noise(streams_of[5], (4, Q, Q, CELLS), 0.15, 0.9, ((3, 512),), jnp.float32),
        "face_proj": noise(streams_of[6], (4, FB, B), B ** -0.5, 0.75, (), jnp.float32),
        "face_lift": noise(streams_of[7], (4, B, FB), FB ** -0.5, 1.25, (), jnp.float32),
        "face_perm": noise(streams_of[8], (3, FB, FB), FB ** -0.5, 1.25, (), jnp.float32),
        "point_proj": noise(streams_of[9], (4, NP, B), B ** -0.5, 0.75, (), jnp.float32),
        "point_lift": noise(streams_of[10], (4, B, NP), NP ** -0.5, 0.875, (), jnp.float32),
        "neighbour": set_ends(jax.random.randint(streams_of[11], (4, CELLS), 0, EXT), jax.random.fold_in(streams_of[11], 1), 0, EXT - 1).astype(jnp.int32),
        "face_code": set_ends(jax.random.randint(streams_of[12], (4, CELLS), 0, 12), jax.random.fold_in(streams_of[12], 1), 0, 11).astype(jnp.int32),
        "send_near": set_ends(jax.random.randint(streams_of[13], (4 * DEVICES, HALO), 0, CELLS_DEV), jax.random.fold_in(streams_of[13], 1), 0, CELLS_DEV - 1).astype(jnp.int32),
        "send_strike": set_ends(jax.random.randint(streams_of[14], (2 * DEVICES, GHALO), 0, CELLS_DEV), jax.random.fold_in(streams_of[14], 1), 0, CELLS_DEV - 1).astype(jnp.int32),
        "fault_minus": set_ends(jax.random.randint(streams_of[15], (FAULTS,), 0, 4 * CELLS_DEV), jax.random.fold_in(streams_of[15], 1), 0, (4 * CELLS_DEV) - 1).astype(jnp.int32),
        "fault_send": draw_fault_send(jax.random.fold_in(streams_of[23], 71), 0),
        "fault_plus": draw_fault_plus(jax.random.fold_in(streams_of[23], 71), 0),
        "fault_live": jax.vmap(lambda own: ragged(own, N_DOM, FAULT_MEAN * N_DOM, FAULT_DEV, 2))(jax.random.split(streams_of[18], N_GROUP)).reshape((N_GROUP, N_DOM)).astype(jnp.int32),
        "normal_load": jnp.clip(jnp.exp(math.log(8.0) - 2.0794415 * jax.random.uniform(streams_of[19], (FAULTS,), jnp.float32) ** block_scale(streams_of[19], (FAULTS,), ((0, 512),), -0.2, 0.2)), 1.0, 8.0),
        "shear_load": noise(streams_of[20], (FAULTS,), 1.0, 4.0, ((0, 512),), jnp.float32),
        "direct_effect": jnp.clip(jnp.exp(math.log(0.6) - 1.0986123 * jax.random.uniform(streams_of[21], (FAULTS,), jnp.float32) ** block_scale(streams_of[21], (FAULTS,), ((0, 512),), -0.2, 0.2)), 0.2, 0.6),
        "state_var": jnp.clip(1.5 * jax.random.uniform(streams_of[22], (FAULTS,), jnp.float32) ** block_scale(streams_of[22], (FAULTS,), ((0, 512),), -0.2, 0.2), 0.0, 1.5),
    }


HIGHEST = lax.Precision.HIGHEST
GAUSS_POINTS = np.array([-0.932469514203152, -0.6612093864662645, -0.2386191860831909, 0.2386191860831909, 0.6612093864662645, 0.932469514203152])
GAUSS_MASSES = np.array([0.1713244923791704, 0.3607615730481386, 0.467913934572691, 0.467913934572691, 0.3607615730481386, 0.1713244923791704])

def time_table():
    gauss_nodes = 0.5 * (GAUSS_POINTS + 1.0)
    powers = np.array([[gauss_nodes[t] ** k / math.factorial(k) for k in range(NDER)] for t in range(NT)])
    return (jnp.asarray(powers, jnp.float32), jnp.asarray(0.5 * GAUSS_MASSES, jnp.float32))

def inverse_sinh(value):
    magnitude = jnp.abs(value)
    result = jnp.log(magnitude + jnp.sqrt(1.0 + value * value))
    return jnp.where(value < 0, -result, result)

def cell_mix(matrix, field):
    total = matrix[:, 0, None, :] * field[0][None, :, :]
    for q in range(1, matrix.shape[1]):
        total = total + matrix[:, q, None, :] * field[q][None, :, :]
    return total

def cauchy_kovalewski(cell_dofs, star_matrix, stiffness):
    current = cell_dofs
    orders_list = [cell_dofs]
    for degree in range(NDER - 1):
        following = jnp.zeros_like(cell_dofs)
        for j in range(3):
            moved_term = jnp.einsum('qbn,bc->qcn', current, stiffness[j], precision=HIGHEST)
            following = following + cell_mix(star_matrix[j], moved_term)
        current = following
        orders_list.append(current)
    return jnp.stack(orders_list)

def integrate(derivs):
    total = derivs[0]
    for degree in range(1, NDER):
        total = total + derivs[degree] / math.factorial(degree + 1)
    return total

def volume_term(integral, star_matrix, volume_kernel):
    result = jnp.zeros_like(integral)
    for j in range(3):
        moved_term = jnp.einsum('qbn,bc->qcn', integral, volume_kernel[j], precision=HIGHEST)
        result = result + cell_mix(star_matrix[j], moved_term)
    return result

def local_flux(integral, flux_local, face_proj, face_lift):
    result = jnp.zeros_like(integral)
    for i in range(4):
        face_trace = jnp.einsum('qbn,fb->qfn', integral, face_proj[i], precision=HIGHEST)
        solved = cell_mix(flux_local[i], face_trace)
        result = result + jnp.einsum('pfn,bf->pbn', solved, face_lift[i], precision=HIGHEST)
    return result

def neighbour_flux(extended, neighbour, face_code, flux_neigh, face_proj, face_perm, face_lift):
    ext_count = extended.shape[2]
    projected = jnp.einsum('qbn,jfb->qfjn', extended, face_proj, precision=HIGHEST)
    projected = projected.reshape(projected.shape[0], projected.shape[1], 4 * ext_count)
    result = jnp.zeros((extended.shape[0], face_lift.shape[1], neighbour.shape[1]), jnp.float32)
    for i in range(4):
        code_row = face_code[i]
        flat_index = code_row // 3 * ext_count + neighbour[i]
        picked = jnp.take(projected, flat_index, axis=2)
        turned = jnp.einsum('qgn,hfg->hqfn', picked, face_perm, precision=HIGHEST)
        choose = ((code_row % 3)[None, :] == jnp.arange(3, dtype=jnp.int32)[:, None]).astype(jnp.float32)
        oriented = lax.optimization_barrier(jnp.sum(turned * choose[:, None, None, :], axis=0))
        solved = cell_mix(flux_neigh[i], oriented)
        result = result + jnp.einsum('pfn,bf->pbn', solved, face_lift[i], precision=HIGHEST)
    return result

def select_quantities(derivs):
    return jnp.stack([derivs[:, 0], derivs[:, 3], derivs[:, 7]], axis=1)

def fault_traces(chosen, face_ids, point_proj):
    powers, gauss_weights = time_table()
    in_time = jnp.einsum('tk,kqbn->tqbn', powers, chosen, precision=HIGHEST)
    all_faces = jnp.einsum('tqbn,ipb->itqpn', in_time, point_proj, precision=HIGHEST)
    choose = (face_ids[None, :] == jnp.arange(4, dtype=jnp.int32)[:, None]).astype(jnp.float32)
    return lax.optimization_barrier(jnp.sum(all_faces * choose[:, None, None, None, :], axis=0))

def friction(minus_side, plus_side, normal_load, shear_load, direct_effect, state_var):
    strength = jnp.maximum(normal_load - 0.5 * (minus_side[:, 0] + plus_side[:, 0]), 0.0)
    locked = shear_load + 0.5 * (minus_side[:, 1] + plus_side[:, 1]) + 0.5 * (plus_side[:, 2] - minus_side[:, 2])
    factor = 0.5 * jnp.exp(state_var / direct_effect)
    scaled = strength * direct_effect
    slip_now = jnp.zeros_like(locked)
    for m in range(NEWTON):
        argument = factor * slip_now
        residue = locked - 0.5 * slip_now - scaled * inverse_sinh(argument)
        slope = -0.5 - scaled * factor / jnp.sqrt(1.0 + argument * argument)
        slip_now = slip_now - residue / slope
    stress = locked - shear_load - 0.5 * slip_now
    return (slip_now, stress)

def fault_amount(stress, side_trace, live_mask):
    powers, gauss_weights = time_table()
    return jnp.einsum('t,tpn->pn', gauss_weights, stress - side_trace[:, 1], precision=HIGHEST) * live_mask

def fault_lift(amount, cell_ids, face_ids, flux_local, point_lift, orient_sign):
    columns = jnp.take(flux_local, cell_ids, axis=3)
    mixed = columns[:, :, 3, :] + orient_sign * columns[:, :, 7, :]
    choose = (face_ids[None, :] == jnp.arange(4, dtype=jnp.int32)[:, None]).astype(jnp.float32)
    weight = lax.optimization_barrier(jnp.sum(mixed * choose[:, None, :], axis=0))
    lifted_all = jnp.einsum('ibp,pf->ibf', point_lift, amount, precision=HIGHEST)
    lifted = lax.optimization_barrier(jnp.sum(lifted_all * choose[:, None, :], axis=0))
    return weight[:, None, :] * lifted[None, :, :]

def reference(cell_dofs, star_matrix, stiffness, volume_kernel, flux_local, flux_neigh, face_proj, face_lift, face_perm, point_proj, point_lift, neighbour, face_code, send_near, send_strike, fault_minus, fault_send, fault_plus, fault_live, normal_load, shear_load, direct_effect, state_var):
    device_total = N_GROUP * N_DOM
    peer_slots = FAULT_DEV // 4
    offset_table = jnp.array([-2, -1, 0, 1, 2], dtype=jnp.int32)

    def device_slice(array, device, width):
        return lax.dynamic_slice_in_dim(array, device * width, width, axis=array.ndim - 1)

    def integral_of(device):
        derivs = cauchy_kovalewski(device_slice(cell_dofs, device, CELLS_DEV), device_slice(star_matrix, device, CELLS_DEV), stiffness)
        return integrate(derivs)
    integrals = lax.map(integral_of, jnp.arange(device_total, dtype=jnp.int32))

    def update_of(device):
        group_id = device // N_DOM
        rank_id = device % N_DOM
        own_dofs = device_slice(cell_dofs, device, CELLS_DEV)
        own_star = device_slice(star_matrix, device, CELLS_DEV)
        own_flux = device_slice(flux_local, device, CELLS_DEV)
        integral = integrals[device]
        blocks = [integral]
        for k, offset in enumerate((-2, -1, 1, 2)):
            source = rank_id - offset
            inside = ((source >= 0) & (source < N_DOM)).astype(jnp.float32)
            sender = group_id * N_DOM + jnp.clip(source, 0, N_DOM - 1)
            listed = send_near[sender * 4 + k]
            blocks.append(jnp.take(integrals[sender], listed, axis=2) * inside)
        for k, offset in enumerate((-1, 1)):
            source = group_id - offset
            inside = ((source >= 0) & (source < N_GROUP)).astype(jnp.float32)
            sender = jnp.clip(source, 0, N_GROUP - 1) * N_DOM + rank_id
            listed = send_strike[sender * 2 + k]
            blocks.append(jnp.take(integrals[sender], listed, axis=2) * inside)
        extended = jnp.concatenate(blocks, axis=2)
        updated = own_dofs + volume_term(integral, own_star, volume_kernel)
        updated = updated - local_flux(integral, own_flux, face_proj, face_lift)
        updated = updated - neighbour_flux(extended, device_slice(neighbour, device, CELLS_DEV), device_slice(face_code, device, CELLS_DEV), device_slice(flux_neigh, device, CELLS_DEV), face_proj, face_perm, face_lift)
        minus_code = device_slice(fault_minus, device, FAULT_DEV)
        minus_cells = minus_code // 4
        minus_faces = minus_code % 4
        minus_derivs = cauchy_kovalewski(jnp.take(own_dofs, minus_cells, axis=2), jnp.take(own_star, minus_cells, axis=3), stiffness)
        minus_side = fault_traces(select_quantities(minus_derivs), minus_faces, point_proj)
        plus_code = device_slice(fault_plus, device, FAULT_DEV)
        plus_slot = plus_code // 4
        plus_faces = plus_code % 4
        list_id = plus_slot // peer_slots
        source = jnp.clip(rank_id - jnp.take(offset_table, list_id), 0, N_DOM - 1)
        sender = group_id * N_DOM + source
        listed = fault_send[sender * 5 + list_id, plus_slot % peer_slots]
        plus_global = sender * CELLS_DEV + listed // 4
        plus_derivs = cauchy_kovalewski(jnp.take(cell_dofs, plus_global, axis=2), jnp.take(star_matrix, plus_global, axis=3), stiffness)
        plus_side = fault_traces(select_quantities(plus_derivs), plus_faces, point_proj)
        live_mask = (jnp.arange(FAULT_DEV, dtype=jnp.int32) < fault_live[group_id, rank_id]).astype(jnp.float32)
        slip_now, stress = friction(minus_side, plus_side, device_slice(normal_load, device, FAULT_DEV), device_slice(shear_load, device, FAULT_DEV), device_slice(direct_effect, device, FAULT_DEV), device_slice(state_var, device, FAULT_DEV))
        minus_amount = fault_amount(stress, minus_side, live_mask)
        plus_amount = fault_amount(stress, plus_side, live_mask)
        minus_term = fault_lift(minus_amount, minus_cells, minus_faces, own_flux, point_lift, 1.0)
        updated = updated.at[:, :, minus_cells].add(minus_term)
        return (updated, slip_now * live_mask, plus_amount, plus_global, plus_faces)
    updated, slip_all, plus_amount, plus_global, plus_faces = lax.map(update_of, jnp.arange(device_total, dtype=jnp.int32))

    def plus_term_of(device):
        return fault_lift(plus_amount[device], plus_global[device], plus_faces[device], flux_local, point_lift, -1.0)
    plus_terms = lax.map(plus_term_of, jnp.arange(device_total, dtype=jnp.int32))
    new_dofs = jnp.transpose(updated, (1, 2, 0, 3)).reshape(Q, B, CELLS)
    flat_terms = jnp.transpose(plus_terms, (1, 2, 0, 3)).reshape(Q, B, FAULTS)
    new_dofs = new_dofs.at[:, :, plus_global.reshape(FAULTS)].add(flat_terms)
    slip_rate = jnp.transpose(slip_all, (1, 2, 0, 3)).reshape(NT, NP, FAULTS)
    return (new_dofs, slip_rate)
```

```python
import functools
import math

import jax
import jax.numpy as jnp
import numpy as np
from jax import lax
from jax.experimental import pallas as pl
from jax.experimental.pallas import tpu as pltpu
from jax.sharding import PartitionSpec as P

Q = 9
B = 56
FB = 21
FP = 24
NP = 49
NT = 6
NDER = 6
NEWTON = 4
N = 256
SLOTS = 128
LIST = 32
HALO = 16
FROWS = 13 * B
f32 = jnp.float32
bf16 = jnp.bfloat16
i32 = jnp.int32

GAUSS_POINTS = np.array(
    [
        -0.932469514203152,
        -0.6612093864662645,
        -0.2386191860831909,
        0.2386191860831909,
        0.6612093864662645,
        0.932469514203152,
    ]
)
GAUSS_MASSES = np.array(
    [
        0.1713244923791704,
        0.3607615730481386,
        0.467913934572691,
        0.467913934572691,
        0.3607615730481386,
        0.1713244923791704,
    ]
)
NODES = 0.5 * (GAUSS_POINTS + 1.0)
POWERS = [[float(NODES[t] ** k / math.factorial(k)) for k in range(NDER)] for t in range(NT)]
MASSES = [float(0.5 * w) for w in GAUSS_MASSES]
FAULT_OFFSETS = (-2, -1, 0, 1, 2)
NEAR_OFFSETS = (-2, -1, 1, 2)
STRIKE_OFFSETS = (-1, 1)

INPUTS = (
    ["cell", "star", "stiff", "volk", "fl", "fn", "proj", "lift", "perm", "pproj", "plift"]
    + ["neigh", "code", "near", "strike", "fminus", "fsend", "fplus", "live"]
    + ["nload", "sload", "deff", "svar"]
)
SCRATCH = dict(
    d0=pltpu.VMEM((NDER, 5, B, N), f32),
    d1=pltpu.VMEM((NDER, 5, B, N), f32),
    y0=pltpu.VMEM((5, 3 * B, N), f32),
    y1=pltpu.VMEM((5, 3 * B, N), f32),
    v0=pltpu.VMEM((Q, 3 * B + 4 * FP, 128), f32),
    v1=pltpu.VMEM((Q, 3 * B + 4 * FP, 128), f32),
    ig=pltpu.VMEM((Q * B, N), f32),
    lf=pltpu.VMEM((Q, B, N), f32),
    so=pltpu.VMEM((Q, 4 * FP, N), f32),
    ori=pltpu.VMEM((Q, 4 * FP, N), f32),
    a=pltpu.VMEM((NDER, 3 * B, N), f32),
    gm=pltpu.VMEM((NDER, 3 * B, SLOTS), f32),
    pk=pltpu.VMEM((NDER, 2 * B, SLOTS), f32),
    town=pltpu.VMEM((Q * 2 * FP, 4 * N), bf16),
    thalo=pltpu.VMEM((Q * 2 * FP, 4 * 128), bf16),
    pick=pltpu.VMEM((4, Q * 2 * FP, N), f32),
    z=pltpu.VMEM((8, B, N), f32),
    hs=pltpu.VMEM((96, 512), f32),
    hr=pltpu.VMEM((128, 512), f32),
    fs=pltpu.VMEM((NDER, 160, 128), f32),
    fr=pltpu.VMEM((NDER, 160, 128), f32),
    bs=pltpu.VMEM((160, 128), f32),
    br=pltpu.VMEM((256, 128), f32),
    wf=pltpu.VMEM((3 * B + 4 * FP, 384), f32),
    w1=pltpu.VMEM((3 * B, 3 * B), bf16),
    w2=pltpu.VMEM((3 * B + 4 * FP, 3 * B), bf16),
    wp=pltpu.VMEM((3 * FP, 3 * FP), bf16),
    wl=pltpu.VMEM((B, 12 * FP), bf16),
    wq=pltpu.VMEM((4 * B, 3 * B), bf16),
    wz=pltpu.VMEM((4 * B, 3 * B), bf16),
    in_sem=pltpu.SemaphoreType.DMA((23,)),
    fault_send_sem=pltpu.SemaphoreType.DMA((NDER, 4)),
    fault_recv_sem=pltpu.SemaphoreType.DMA((NDER, 4)),
    send_sem=pltpu.SemaphoreType.DMA((10,)),
    recv_sem=pltpu.SemaphoreType.DMA((10,)),
)


def rounded(x):
    return x.astype(bf16).astype(f32)


def split_rows(x):
    hi = rounded(x)
    return jnp.concatenate([hi, x - hi, hi], axis=0).astype(bf16)


def halves(x):
    hi = x.astype(bf16)
    return hi, (x - hi.astype(f32)).astype(bf16)


def dot(a, b):
    return jnp.dot(a, b, preferred_element_type=f32)


def dot_nt(a, b):
    return lax.dot_general(a, b, (((1,), (1,)), ((), ())), preferred_element_type=f32)


def iota(shape, dim):
    return lax.broadcasted_iota(i32, shape, dim)


def onehot(cond):
    return jnp.where(cond, 1.0, 0.0).astype(bf16)


def column(row):
    return jnp.broadcast_to(row.astype(f32), (128, 128)).T.astype(i32)


def wide(x):
    return jnp.concatenate([x, x], axis=1)


def put3(ref, row, cols, x):
    hi = rounded(x)
    lo = x - hi
    for c, part in zip(cols, (hi, hi, lo)):
        ref[row : row + x.shape[0], c : c + x.shape[1]] = part


def weave(*groups):
    steps = []
    for group in groups:
        steps += [((n + 0.5) / len(group), step) for n, step in enumerate(group)]
    for place, step in sorted(steps, key=lambda item: item[0]):
        step()


def mix27(star, tile, half, emit):
    lanes = slice(half * 128, half * 128 + 128)
    tiles = [[tile(j, q) for q in range(Q)] for j in range(3)]
    for p in range(Q):
        parts = []
        for j in range(3):
            acc = star[p, 0, j : j + 1, lanes] * tiles[j][0]
            for q in range(1, Q):
                acc = acc + star[p, q, j : j + 1, lanes] * tiles[j][q]
            parts.append(acc)
        emit(p, lanes, (parts[0] + parts[1]) + parts[2])


def mix9(flux, i, half, tile, dst, row, add):
    lanes = slice(half * 128, half * 128 + 128)
    tiles = [tile(q) for q in range(Q)]
    for p in range(Q):
        acc = flux[p, 0, i : i + 1, lanes] * tiles[0]
        for q in range(1, Q):
            acc = acc + flux[p, q, i : i + 1, lanes] * tiles[q]
        if add:
            acc = acc + dst[p, row : row + 8, lanes]
        dst[p, row : row + 8, lanes] = acc


def kernel(n_group, n_dom, *refs):
    names = ["u", "sl"] + INPUTS + list(SCRATCH)
    hbm = dict(zip(INPUTS, refs))
    r = dict(zip(names, refs[len(INPUTS) :]))
    cell, star, fl, fn = (r[k] for k in ("cell", "star", "fl", "fn"))
    dh, yh, vh = (r["d0"], r["d1"]), (r["y0"], r["y1"]), (r["v0"], r["v1"])
    ig, u, lf, so, ori, a = (r[k] for k in ("ig", "u", "lf", "so", "ori", "a"))
    gm, pk, town, thalo, pick, z = (r[k] for k in ("gm", "pk", "town", "thalo", "pick", "z"))
    hs, hr, fs, fr, bs, br = (r[k] for k in ("hs", "hr", "fs", "fr", "bs", "br"))
    wf, w1, w2, wp, wl, wq, wz = (r[k] for k in ("wf", "w1", "w2", "wp", "wl", "wq", "wz"))
    sl = r["sl"]
    g = lax.axis_index("group")
    me = lax.axis_index("dom")

    first = ["stiff", "cell", "star"]
    late = ["fl", "fn"]
    order = first + [name for name in INPUTS if name not in first + late] + late
    loads = {
        name: pltpu.make_async_copy(hbm[name], r[name], r["in_sem"].at[n])
        for n, name in enumerate(order)
    }
    for name in order:
        loads[name].start()

    def inside(axis, offset):
        at, size = (me, n_dom) if axis == "dom" else (g, n_group)
        target = at + offset
        return jnp.logical_and(target >= 0, target < size), target

    partners = [("dom", o) for o in NEAR_OFFSETS] + [("group", o) for o in STRIKE_OFFSETS]

    barrier = pltpu.get_barrier_semaphore()
    count = 0
    for axis, o in partners:
        ok, target = inside(axis, o)
        count = count + ok.astype(i32)

        @pl.when(ok)
        def _():
            pl.semaphore_signal(
                barrier,
                inc=1,
                device_id={axis: target},
                device_id_type=pl.DeviceIdType.MESH,
            )

    lists = [(s, slice(k * LIST, (k + 1) * LIST), FAULT_OFFSETS[k]) for s, k in enumerate((0, 1, 3, 4))]
    own_list = slice(2 * LIST, 3 * LIST)

    def fault_moves(k):
        return [
            (fs.at[k, rows], fr.at[k, rows], r["fault_send_sem"].at[k, s], r["fault_recv_sem"].at[k, s], "dom", o)
            for s, rows, o in lists
        ]

    halo_moves = []
    for s, (axis, o) in enumerate(partners):
        rows = slice(s * HALO, (s + 1) * HALO)
        halo_moves.append((hs.at[rows], hr.at[rows], r["send_sem"].at[s], r["recv_sem"].at[s], axis, o))
    back_moves = [
        (bs.at[rows], br.at[rows], r["send_sem"].at[6 + s], r["recv_sem"].at[6 + s], "dom", -o)
        for s, rows, o in lists
    ]

    def each(which, action):
        for src, dst, sent, got, axis, o in which:
            ok, target = inside(axis, -o if action == "wait_recv" else o)

            @pl.when(ok)
            def _():
                copy = pltpu.make_async_remote_copy(
                    src_ref=src,
                    dst_ref=dst,
                    send_sem=sent,
                    recv_sem=got,
                    device_id={axis: target},
                    device_id_type=pl.DeviceIdType.MESH,
                )
                getattr(copy, action)()

    for name in order:
        if name not in first + late:
            loads[name].wait()

    sends = r["fsend"][...]
    send_row = [
        jnp.concatenate([sends[k : k + 1, :] for k in range(4)], axis=1),
        jnp.concatenate([sends[4:5, :], jnp.full((1, 96), -4, i32)], axis=1),
    ]
    send_col = jnp.concatenate([column(row) for row in send_row], axis=0)[0:160]
    send_row = jnp.concatenate(send_row, axis=1)
    near = r["near"][...]
    strike = r["strike"][...]
    halo_row = jnp.concatenate(
        [near[k : k + 1, :] for k in range(4)]
        + [strike[k : k + 1, :] for k in range(2)]
        + [jnp.full((1, 32), -1, i32)],
        axis=1,
    )
    halo_col = column(halo_row)[0:96]
    minus_row = r["fminus"][...]
    minus_col = column(minus_row)
    plus_row = r["fplus"][...]
    plus_col = column(lax.shift_right_logical(plus_row, 2))
    send_hot = onehot(lax.shift_right_arithmetic(wide(send_col), 2) == iota((160, N), 1))
    halo_hot = onehot(wide(halo_col) == iota((96, N), 1))
    minus_hot = onehot(lax.shift_right_logical(minus_row, 2) == iota((N, SLOTS), 0))
    plus_hot = onehot(wide(plus_col)[:, 0:160] == iota((SLOTS, 160), 1))
    codes = r["code"][...]
    faces = (codes >= 3).astype(i32) + (codes >= 6).astype(i32) + (codes >= 9).astype(i32)
    turns = codes - 3 * faces
    keys = faces * 384 + r["neigh"][...]

    loads["stiff"].wait()
    put3(wf, 0, (0, 56, 112), jnp.concatenate([r["stiff"][j].T for j in range(3)], axis=0))
    w1[...] = wf[0 : 3 * B, 0 : 3 * B].astype(bf16)
    put3(wf, 0, (0, 56, 112), jnp.concatenate([r["volk"][j].T for j in range(3)], axis=0))
    wf[3 * B :, 0 : 3 * B] = jnp.zeros((4 * FP, 3 * B), f32)
    for i in range(4):
        put3(wf, 3 * B + FP * i, (0, 56, 112), r["proj"][:, i, :])
    w2[...] = wf[:, 0 : 3 * B].astype(bf16)
    wf[...] = jnp.zeros_like(wf)
    for h in range(3):
        put3(wf, FP * h, (0, FP, 2 * FP), r["perm"][h])
    wp[...] = wf[0 : 3 * FP, 0 : 3 * FP].astype(bf16)
    wf[...] = jnp.zeros_like(wf)
    for i in range(4):
        put3(wf, 0, tuple(FP * (i + 4 * s) for s in range(3)), r["lift"][:, i, :].T)
    wl[...] = wf[0:B, 0 : 12 * FP].astype(bf16)
    wf[...] = jnp.zeros_like(wf)
    for i in range(4):
        put3(wf, B * i, (0, 56, 112), r["pproj"][:, i, :])
    wq[...] = wf[0 : 4 * B, 0 : 3 * B].astype(bf16)
    wf[...] = jnp.zeros_like(wf)
    for i in range(4):
        put3(wf, B * i, (0, 56, 112), r["plift"][:, i, :].T)
    wz[...] = wf[0 : 4 * B, 0 : 3 * B].astype(bf16)

    for s, rows, o in lists:
        for ref, offset in ((fr, o), (br, -o)):
            ok, target = inside("dom", -offset)

            @pl.when(jnp.logical_not(ok))
            def _():
                if ref is fr:
                    for k in range(NDER):
                        fr[k, rows] = jnp.zeros((LIST, 128), f32)
                else:
                    br[rows] = jnp.zeros((LIST, 128), f32)

    for s, (axis, o) in enumerate(partners):
        ok, target = inside(axis, -o)

        @pl.when(jnp.logical_not(ok))
        def _():
            hr[s * HALO : (s + 1) * HALO] = jnp.zeros((HALO, 512), f32)

    hr[96:128, :] = jnp.zeros((32, 512), f32)
    br[160:256, :] = jnp.zeros((96, 128), f32)

    loads["cell"].wait()
    for q in range(Q):
        value = cell[q]
        ig[q * B : (q + 1) * B, :] = value
        for half in range(2):
            dh[half][0, q // 2, :, (q % 2) * 128 : (q % 2) * 128 + 128] = value[
                :, half * 128 : half * 128 + 128
            ]
    a[0, 0:B] = cell[0]
    a[0, B : 2 * B] = cell[3] + cell[7]
    a[0, 2 * B :] = cell[3] - cell[7]
    loads["star"].wait()

    def moved(k, half):
        def one(pair):
            width = 256 if pair < 4 else 128
            yh[half][pair, :, 0:width] = dot(w1[...], split_rows(dh[half][k, pair, :, 0:width]))

        return [functools.partial(one, pair) for pair in range(5)]

    def mixed(k, half, weight):
        def one(ct):
            held = {}

            def tile(j, q):
                row = j * B + ct * 8
                lane = (q % 2) * 128
                return yh[half][q // 2, row : row + 8, lane : lane + 128]

            def emit(p, lanes, value):
                rows = slice(ct * 8, ct * 8 + 8)
                lane = (p % 2) * 128
                dh[half][k + 1, p // 2, rows, lane : lane + 128] = value
                at = slice(p * B + ct * 8, p * B + ct * 8 + 8)
                ig[at, lanes] = ig[at, lanes] + value * weight
                if p == 0:
                    a[k + 1, rows, lanes] = value
                if p == 3:
                    held[0] = value
                if p == 7:
                    at = slice(B + ct * 8, B + ct * 8 + 8)
                    a[k + 1, at, lanes] = held[0] + value
                    at = slice(2 * B + ct * 8, 2 * B + ct * 8 + 8)
                    a[k + 1, at, lanes] = held[0] - value

            mix27(star, tile, half, emit)

        return [functools.partial(one, ct) for ct in range(7)]

    def payload(k):
        hi, lo = halves(a[k])
        rows = 2 * B
        fs[k, :, 0:rows] = dot_nt(send_hot, hi[0:rows]) + dot_nt(send_hot, lo[0:rows])
        fs[k, :, rows:] = jnp.zeros((160, 128 - rows), f32)
        gm[k] = dot(hi, minus_hot) + dot(lo, minus_hot)

    def post(k):
        each(fault_moves(k), "start")
        fr[k, own_list] = fs[k, own_list]

    def derive(k, weight):
        weight = weight / (k + 2).astype(f32)
        payload(k)
        weave(moved(k, 1), mixed(k, 0, weight))

        @pl.when(k == 2)
        def _():
            pl.semaphore_wait(barrier, count)
            post(0)
            post(1)
            post(2)

        @pl.when(k == 3)
        def _():
            post(3)

        weave(moved(k + 1, 0), mixed(k, 1, weight))
        return weight

    def spread(half):
        lanes = slice(half * 128, half * 128 + 128)

        def one(q):
            vh[half][q] = dot(w2[...], split_rows(ig[q * B : (q + 1) * B, lanes]))

        return [functools.partial(one, q) for q in range(Q)]

    weave(moved(0, 0))
    lax.fori_loop(0, NDER - 2, derive, jnp.float32(1.0))
    last = NDER - 2
    weight = jnp.float32(1.0 / math.factorial(NDER))
    payload(last)
    weave(moved(last, 1), mixed(last, 0, weight))
    post(last)
    weave(spread(0), mixed(last, 1, weight))
    payload(last + 1)
    i_hi, i_lo = halves(ig[...])
    hs[:, 0 : Q * B] = dot_nt(halo_hot, i_hi) + dot_nt(halo_hot, i_lo)
    hs[:, Q * B : 512] = jnp.zeros((96, 512 - Q * B), f32)
    post(last + 1)
    each(halo_moves, "start")
    send_cells = lax.shift_right_arithmetic(send_row, 2)
    shear_hot = jnp.concatenate([onehot(send_cells == iota((N, 256), 0)), minus_hot], axis=1)
    s_hi, s_lo = i_hi[3 * B : 4 * B], i_lo[3 * B : 4 * B]
    face_row = jnp.concatenate([minus_row & 3, plus_row & 3], axis=1)

    def projected(x, row):
        full = dot(wq[...], split_rows(x))
        best = full[3 * B :]
        for i in range(3):
            best = jnp.where(row == i, full[i * B : (i + 1) * B], best)
        return best

    shear = projected(
        dot(s_hi, shear_hot) + dot(s_lo, shear_hot),
        jnp.concatenate([send_row & 3, minus_row & 3], axis=1),
    )
    psi, m_w = shear[:, 0:256], shear[:, 256:]

    loads["fl"].wait()

    def local(half):
        def inner(ct):
            def tile(j, q):
                row = j * B + ct * 8
                return vh[half][q, row : row + 8, :]

            def emit(p, lanes, value):
                rows = slice(ct * 8, ct * 8 + 8)
                u[p, rows, lanes] = cell[p, rows, lanes] + value

            mix27(star, tile, half, emit)

        def face(row):
            mix9(
                fl, row // FP, half, lambda q: vh[half][q, 3 * B + row : 3 * B + row + 8, :], so, row, False
            )

        return [functools.partial(inner, ct) for ct in range(7)] + [
            functools.partial(face, row) for row in range(0, 4 * FP, 8)
        ]

    def table(half):
        for q in range(Q):
            for j in range(4):
                block = vh[half][q, 3 * B + FP * j : 3 * B + FP * (j + 1), :]
                hi = rounded(block)
                town[
                    q * 2 * FP : (q + 1) * 2 * FP, j * N + half * 128 : j * N + half * 128 + 128
                ] = jnp.concatenate([hi, block - hi], axis=0).astype(bf16)

    def arrived(k):
        hi, lo = halves(fr[k])
        gt = (dot(plus_hot, hi) + dot(plus_hot, lo)).T
        for n in range(2):
            both = jnp.concatenate(
                [gm[k, 2 * n * B : 2 * n * B + B], gt[n * B : (n + 1) * B]], axis=1
            )
            best = projected(both, face_row)
            pk[k, n * B : (n + 1) * B] = best[:, 0:SLOTS] + best[:, SLOTS:]

    def near_pick(i):
        hot = jnp.concatenate(
            [onehot(keys[i : i + 1, :] == iota((N, N), 0) + 384 * j) for j in range(4)], axis=0
        )
        pick[i] = dot(town[...], hot)
    weave(local(0), spread(1))
    table(0)
    table(1)
    for k in range(NDER - 1):
        each(fault_moves(k), "wait_recv")
    weave(local(1), [functools.partial(arrived, k) for k in range(NDER - 1)] + [functools.partial(near_pick, i) for i in range(4)])

    each(fault_moves(NDER - 1), "wait_recv")
    each(halo_moves, "wait_recv")
    arrived(NDER - 1)
    alive = (iota((1, SLOTS), 1) < r["live"][...]).astype(f32)
    nload, sload, deff = r["nload"][...], r["sload"][...], r["deff"][...]
    factor = 0.5 * jnp.exp(r["svar"][...] / deff)
    total = jnp.zeros((B, SLOTS), f32)
    for t in range(NT):
        normal = pk[0, 0:B]
        tangent = pk[0, B:]
        for k in range(1, NDER):
            normal = normal + POWERS[t][k] * pk[k, 0:B]
            tangent = tangent + POWERS[t][k] * pk[k, B:]
        strength = jnp.maximum(nload - 0.5 * normal, 0.0)
        locked = sload + 0.5 * tangent
        scaled = strength * deff
        curve = scaled * factor
        now = locked / (0.5 + curve)
        for m in range(NEWTON - 1):
            arg = factor * now
            root = jnp.sqrt(1.0 + arg * arg)
            mag = jnp.log(jnp.abs(arg) + root)
            asinh = jnp.where(arg < 0, -mag, mag)
            residue = locked - 0.5 * now - scaled * asinh
            slope = -0.5 - curve / root
            now = now - residue / slope
        sl[t] = (now * alive)[0:NP]
        total = total + MASSES[t] * (locked - sload - 0.5 * now)
    am = (total - m_w) * alive
    ap = jnp.where(iota((B, SLOTS), 0) == NP, alive, total * alive)

    entry_hot = onehot(lax.shift_right_logical(plus_row, 2) == iota((160, SLOTS), 0))
    b_hi, b_lo = halves(jnp.concatenate([ap, jnp.zeros((128 - B, SLOTS), f32)], axis=0))
    bs[...] = dot_nt(entry_hot, b_hi) + dot_nt(entry_hot, b_lo)
    each(back_moves, "start")
    br[own_list, :] = bs[own_list, :]

    ht = hr[...].T
    for q in range(Q):
        full = dot(w2[3 * B :, :], split_rows(ht[q * B : (q + 1) * B, :]))
        for j in range(4):
            block = full[FP * j : FP * (j + 1), :]
            hi = rounded(block)
            thalo[q * 2 * FP : (q + 1) * 2 * FP, j * 128 : (j + 1) * 128] = jnp.concatenate(
                [hi, block - hi], axis=0
            ).astype(bf16)
    loads["fn"].wait()

    def turned(i):
        hot = jnp.concatenate(
            [onehot(keys[i : i + 1, :] == iota((128, N), 0) + (384 * j + N)) for j in range(4)],
            axis=0,
        )
        both = pick[i] + dot(thalo[...], hot)
        for q in range(Q):
            hi = both[q * 2 * FP : q * 2 * FP + FP]
            lo = both[q * 2 * FP + FP : (q + 1) * 2 * FP]
            full = dot(wp[...], jnp.concatenate([hi, lo, hi], axis=0).astype(bf16))
            best = full[2 * FP :]
            for h in range(2):
                best = jnp.where(turns[i : i + 1, :] == h, full[h * FP : (h + 1) * FP], best)
            ori[q, i * FP : (i + 1) * FP, :] = best

    def far(i):
        def one(row, half):
            lanes = slice(half * 128, half * 128 + 128)
            mix9(fn, i, half, lambda q: ori[q, row : row + 8, lanes], so, row, True)

        return [
            functools.partial(one, row, half)
            for row in range(i * FP, (i + 1) * FP, 8)
            for half in range(2)
        ]

    weave([functools.partial(turned, 0)])
    for i in range(3):
        weave([functools.partial(turned, i + 1)], far(i))

    each(back_moves, "wait_recv")
    am_hi, am_lo = halves(am)
    back = br[...].T
    back = back[0:B] - back[NP : NP + 1] * psi
    bt_hi, bt_lo = halves(back[:, 0:160])

    def lifted(i):
        own_hot = onehot(wide(minus_col) == iota((SLOTS, N), 1) * 4 + i)
        far_hot = onehot(wide(send_col) == iota((160, N), 1) * 4 + i)
        e_m = dot(am_hi, own_hot) + dot(am_lo, own_hot)
        e_p = dot(bt_hi, far_hot) + dot(bt_lo, far_hot)
        w = wz[i * B : (i + 1) * B, :]
        z[i] = dot(w, split_rows(e_m + e_p))
        z[4 + i] = dot(w, split_rows(e_m - e_p))

    weave([functools.partial(lifted, i) for i in range(4)], far(3))
    lf[0] = dot(wl[...], split_rows(so[0]))
    for p in range(Q):
        if p + 1 < Q:
            lf[p + 1] = dot(wl[...], split_rows(so[p + 1]))
        for ct in range(7):
            rows = slice(ct * 8, ct * 8 + 8)
            for half in range(2):
                lanes = slice(half * 128, half * 128 + 128)
                acc = u[p, rows, lanes] - lf[p, rows, lanes]
                for i in range(4):
                    acc = acc + fl[p, 3, i : i + 1, lanes] * z[i, rows, lanes]
                    acc = acc + fl[p, 7, i : i + 1, lanes] * z[4 + i, rows, lanes]
                u[p, rows, lanes] = acc
    for k in range(NDER):
        each(fault_moves(k), "wait_send")
    each(halo_moves, "wait_send")
    each(back_moves, "wait_send")


def per_device(n_group, n_dom, *args):
    args = list(args)
    for at in (1, 4, 5):
        args[at] = args[at].transpose(1, 2, 0, 3)
    for at in (6, 9):
        args[at] = args[at].transpose(1, 0, 2)
    for at in (7, 10):
        args[at] = args[at].transpose(2, 0, 1)
    for at in (15, 17, 19, 20, 21, 22):
        args[at] = args[at].reshape(1, SLOTS)
    return pl.pallas_call(
        functools.partial(kernel, n_group, n_dom),
        out_shape=(pltpu.VMEM((Q, B, N), f32), pltpu.VMEM((NT, NP, SLOTS), f32)),
        in_specs=[pl.BlockSpec(memory_space=pl.ANY)] * len(args),
        out_specs=(pl.BlockSpec(memory_space=pltpu.VMEM),) * 2,
        scratch_shapes=[pltpu.VMEM(x.shape, x.dtype) for x in args] + list(SCRATCH.values()),
        compiler_params=pltpu.CompilerParams(
            collective_id=0, has_side_effects=True, vmem_limit_bytes=56 << 20
        ),
        name="ader_step",
    )(*args)


def solution(mesh):
    both = ("group", "dom")
    return jax.shard_map(
        functools.partial(per_device, mesh.shape["group"], mesh.shape["dom"]),
        mesh=mesh,
        in_specs=(
            P(None, None, both),
            P(None, None, None, both),
            P(),
            P(),
            P(None, None, None, both),
            P(None, None, None, both),
            P(),
            P(),
            P(),
            P(),
            P(),
            P(None, both),
            P(None, both),
            P(both, None),
            P(both, None),
            P(both),
            P(both, None),
            P(both),
            P("group", "dom"),
            P(both),
            P(both),
            P(both),
            P(both),
        ),
        out_specs=(P(None, None, both), P(None, None, both)),
        check_vma=False,
    )
```

```python
import functools
import math

import jax
import jax.numpy as jnp
import numpy as np
from jax import lax
from jax.experimental import pallas as pl
from jax.experimental.pallas import tpu as pltpu
from jax.sharding import PartitionSpec as P

Q = 9
B = 56
FB = 21
FP = 24
NP = 49
NT = 6
NDER = 6
NEWTON = 4
N = 256
SLOTS = 128
LIST = 32
HALO = 16
FROWS = 13 * B
f32 = jnp.float32
bf16 = jnp.bfloat16
i32 = jnp.int32

GAUSS_POINTS = np.array(
    [
        -0.932469514203152,
        -0.6612093864662645,
        -0.2386191860831909,
        0.2386191860831909,
        0.6612093864662645,
        0.932469514203152,
    ]
)
GAUSS_MASSES = np.array(
    [
        0.1713244923791704,
        0.3607615730481386,
        0.467913934572691,
        0.467913934572691,
        0.3607615730481386,
        0.1713244923791704,
    ]
)
NODES = 0.5 * (GAUSS_POINTS + 1.0)
POWERS = [[float(NODES[t] ** k / math.factorial(k)) for k in range(NDER)] for t in range(NT)]
MASSES = [float(0.5 * w) for w in GAUSS_MASSES]
FAULT_OFFSETS = (-2, -1, 0, 1, 2)
NEAR_OFFSETS = (-2, -1, 1, 2)
STRIKE_OFFSETS = (-1, 1)

INPUTS = (
    ["cell", "star", "stiff", "volk", "fl", "fn", "proj", "lift", "perm", "pproj", "plift"]
    + ["neigh", "code", "near", "strike", "fminus", "fsend", "fplus", "live"]
    + ["nload", "sload", "deff", "svar"]
)
SCRATCH = dict(
    d0=pltpu.VMEM((NDER, 5, B, N), f32),
    d1=pltpu.VMEM((NDER, 5, B, N), f32),
    y0=pltpu.VMEM((5, 3 * B, N), f32),
    y1=pltpu.VMEM((5, 3 * B, N), f32),
    v0=pltpu.VMEM((Q, 3 * B + 4 * FP, 128), f32),
    v1=pltpu.VMEM((Q, 3 * B + 4 * FP, 128), f32),
    ig=pltpu.VMEM((Q * B, N), f32),
    so=pltpu.VMEM((Q, 4 * FP, N), f32),
    ori=pltpu.VMEM((Q, 4 * FP, N), f32),
    a=pltpu.VMEM((NDER, 3 * B, N), f32),
    gm=pltpu.VMEM((NDER, 3 * B, SLOTS), f32),
    pk=pltpu.VMEM((NDER, 2 * B, SLOTS), f32),
    town=pltpu.VMEM((Q * 2 * FP, 4 * N), bf16),
    thalo=pltpu.VMEM((Q * 2 * FP, 4 * 128), bf16),
    pick=pltpu.VMEM((4, Q * 2 * FP, N), f32),
    z=pltpu.VMEM((8, B, N), f32),
    hs=pltpu.VMEM((96, 512), f32),
    hr=pltpu.VMEM((128, 512), f32),
    fs=pltpu.VMEM((NDER, 160, 128), f32),
    fr=pltpu.VMEM((NDER, 160, 128), f32),
    bs=pltpu.VMEM((160, 128), f32),
    br=pltpu.VMEM((256, 128), f32),
    wf=pltpu.VMEM((3 * B + 4 * FP, 384), f32),
    w1=pltpu.VMEM((3 * B, 3 * B), bf16),
    w2=pltpu.VMEM((3 * B + 4 * FP, 3 * B), bf16),
    wp=pltpu.VMEM((3 * FP, 3 * FP), bf16),
    wl=pltpu.VMEM((B, 12 * FP), bf16),
    wq=pltpu.VMEM((4 * B, 3 * B), bf16),
    wz=pltpu.VMEM((4 * B, 3 * B), bf16),
    in_sem=pltpu.SemaphoreType.DMA((23,)),
    fault_send_sem=pltpu.SemaphoreType.DMA((2, 4)),
    fault_recv_sem=pltpu.SemaphoreType.DMA((2, 4)),
    send_sem=pltpu.SemaphoreType.DMA((10,)),
    recv_sem=pltpu.SemaphoreType.DMA((10,)),
)


def rounded(x):
    return x.astype(bf16).astype(f32)


def split_rows(x):
    hi = rounded(x)
    return jnp.concatenate([hi, x - hi, hi], axis=0).astype(bf16)


def halves(x):
    hi = x.astype(bf16)
    return hi, (x - hi.astype(f32)).astype(bf16)


def dot(a, b):
    return jnp.dot(a, b, preferred_element_type=f32)


def dot_nt(a, b):
    return lax.dot_general(a, b, (((1,), (1,)), ((), ())), preferred_element_type=f32)


def iota(shape, dim):
    return lax.broadcasted_iota(i32, shape, dim)


def onehot(cond):
    return jnp.where(cond, 1.0, 0.0).astype(bf16)


def column(row):
    return jnp.broadcast_to(row.astype(f32), (128, 128)).T.astype(i32)


def wide(x):
    return jnp.concatenate([x, x], axis=1)


def put3(ref, row, cols, x):
    hi = rounded(x)
    lo = x - hi
    for c, part in zip(cols, (hi, hi, lo)):
        ref[row : row + x.shape[0], c : c + x.shape[1]] = part


def weave(*groups):
    steps = []
    for group in groups:
        steps += [((n + 0.5) / len(group), step) for n, step in enumerate(group)]
    for place, step in sorted(steps, key=lambda item: item[0]):
        step()


def mix27(star, tile, half, emit):
    lanes = slice(half * 128, half * 128 + 128)
    tiles = [[tile(j, q) for q in range(Q)] for j in range(3)]
    for p in range(Q):
        parts = []
        for j in range(3):
            acc = star[p, 0, j : j + 1, lanes] * tiles[j][0]
            for q in range(1, Q):
                acc = acc + star[p, q, j : j + 1, lanes] * tiles[j][q]
            parts.append(acc)
        emit(p, lanes, (parts[0] + parts[1]) + parts[2])


def mix9(flux, i, half, tile, dst, row, add):
    lanes = slice(half * 128, half * 128 + 128)
    tiles = [tile(q) for q in range(Q)]
    for p in range(Q):
        acc = flux[p, 0, i : i + 1, lanes] * tiles[0]
        for q in range(1, Q):
            acc = acc + flux[p, q, i : i + 1, lanes] * tiles[q]
        if add:
            acc = acc + dst[p, row : row + 8, lanes]
        dst[p, row : row + 8, lanes] = acc


def kernel(n_group, n_dom, *refs):
    names = ["u", "sl"] + INPUTS + list(SCRATCH)
    hbm = dict(zip(INPUTS, refs))
    r = dict(zip(names, refs[len(INPUTS) :]))
    cell, star, fl, fn = (r[k] for k in ("cell", "star", "fl", "fn"))
    dh, yh, vh = (r["d0"], r["d1"]), (r["y0"], r["y1"]), (r["v0"], r["v1"])
    ig, u, so, ori, a = (r[k] for k in ("ig", "u", "so", "ori", "a"))
    gm, pk, town, thalo, pick, z = (r[k] for k in ("gm", "pk", "town", "thalo", "pick", "z"))
    hs, hr, fs, fr, bs, br = (r[k] for k in ("hs", "hr", "fs", "fr", "bs", "br"))
    wf, w1, w2, wp, wl, wq, wz = (r[k] for k in ("wf", "w1", "w2", "wp", "wl", "wq", "wz"))
    sl = r["sl"]
    g = lax.axis_index("group")
    me = lax.axis_index("dom")

    large = ["cell", "star", "fl", "fn"]
    order = [name for name in INPUTS if name not in large] + large
    loads = {
        name: pltpu.make_async_copy(hbm[name], r[name], r["in_sem"].at[n])
        for n, name in enumerate(order)
    }
    for name in order:
        loads[name].start()

    def inside(axis, offset):
        at, size = (me, n_dom) if axis == "dom" else (g, n_group)
        target = at + offset
        return jnp.logical_and(target >= 0, target < size), target

    partners = [("dom", o) for o in NEAR_OFFSETS] + [("group", o) for o in STRIKE_OFFSETS]

    barrier = pltpu.get_barrier_semaphore()
    count = 0
    for axis, o in partners:
        ok, target = inside(axis, o)
        count = count + ok.astype(i32)

        @pl.when(ok)
        def _():
            pl.semaphore_signal(
                barrier,
                inc=1,
                device_id={axis: target},
                device_id_type=pl.DeviceIdType.MESH,
            )

    lists = [(s, slice(k * LIST, (k + 1) * LIST), FAULT_OFFSETS[k]) for s, k in enumerate((0, 1, 3, 4))]
    own_list = slice(2 * LIST, 3 * LIST)

    def fault_moves(part):
        orders = (slice(0, 4), slice(4, NDER))[part]
        return [
            (
                fs.at[orders, rows],
                fr.at[orders, rows],
                r["fault_send_sem"].at[part, s],
                r["fault_recv_sem"].at[part, s],
                "dom",
                o,
            )
            for s, rows, o in lists
        ]

    halo_moves = []
    for s, (axis, o) in enumerate(partners):
        rows = slice(s * HALO, (s + 1) * HALO)
        halo_moves.append((hs.at[rows], hr.at[rows], r["send_sem"].at[s], r["recv_sem"].at[s], axis, o))
    back_moves = [
        (bs.at[rows], br.at[rows], r["send_sem"].at[6 + s], r["recv_sem"].at[6 + s], "dom", -o)
        for s, rows, o in lists
    ]

    def each(which, action):
        for axis, o in partners:
            to = -o if action == "wait_recv" else o
            ok, target = inside(axis, to)
            mine = [move for move in which if move[4:] == (axis, o)]
            if not mine:
                continue

            @pl.when(ok)
            def _():
                for src, dst, sent, got, _, _ in mine:
                    copy = pltpu.make_async_remote_copy(
                        src_ref=src,
                        dst_ref=dst,
                        send_sem=sent,
                        recv_sem=got,
                        device_id={axis: target},
                        device_id_type=pl.DeviceIdType.MESH,
                    )
                    getattr(copy, action)()

    for name in order:
        if name not in large:
            loads[name].wait()

    sends = r["fsend"][...]
    send_row = [
        jnp.concatenate([sends[k : k + 1, :] for k in range(4)], axis=1),
        jnp.concatenate([sends[4:5, :], jnp.full((1, 96), -4, i32)], axis=1),
    ]
    send_col = jnp.concatenate([column(row) for row in send_row], axis=0)[0:160]
    send_row = jnp.concatenate(send_row, axis=1)
    near = r["near"][...]
    strike = r["strike"][...]
    halo_row = jnp.concatenate(
        [near[k : k + 1, :] for k in range(4)]
        + [strike[k : k + 1, :] for k in range(2)]
        + [jnp.full((1, 32), -1, i32)],
        axis=1,
    )
    halo_col = column(halo_row)[0:96]
    minus_row = r["fminus"][...]
    minus_col = column(minus_row)
    plus_row = r["fplus"][...]
    plus_col = column(lax.shift_right_logical(plus_row, 2))
    send_hot = onehot(lax.shift_right_arithmetic(wide(send_col), 2) == iota((160, N), 1))
    halo_hot = onehot(wide(halo_col) == iota((96, N), 1))
    minus_hot = onehot(lax.shift_right_logical(minus_row, 2) == iota((N, SLOTS), 0))
    plus_hot = onehot(wide(plus_col)[:, 0:160] == iota((SLOTS, 160), 1))
    codes = r["code"][...]
    faces = (codes >= 3).astype(i32) + (codes >= 6).astype(i32) + (codes >= 9).astype(i32)
    turns = codes - 3 * faces
    near_col = r["neigh"][...]

    def masked(hot, i):
        parts = [
            hot * jnp.broadcast_to(jnp.where(faces[i : i + 1, :] == j, 1.0, 0.0), hot.shape).astype(bf16)
            for j in range(4)
        ]
        return jnp.concatenate(parts, axis=0)


    put3(wf, 0, (0, 56, 112), jnp.concatenate([r["stiff"][j].T for j in range(3)], axis=0))
    w1[...] = wf[0 : 3 * B, 0 : 3 * B].astype(bf16)
    put3(wf, 0, (0, 56, 112), jnp.concatenate([r["volk"][j].T for j in range(3)], axis=0))
    wf[3 * B :, 0 : 3 * B] = jnp.zeros((4 * FP, 3 * B), f32)
    for i in range(4):
        put3(wf, 3 * B + FP * i, (0, 56, 112), r["proj"][:, i, :])
    w2[...] = wf[:, 0 : 3 * B].astype(bf16)
    wf[...] = jnp.zeros_like(wf)
    for h in range(3):
        put3(wf, FP * h, (0, FP, 2 * FP), r["perm"][h])
    wp[...] = wf[0 : 3 * FP, 0 : 3 * FP].astype(bf16)
    wf[...] = jnp.zeros_like(wf)
    for i in range(4):
        put3(wf, 0, tuple(FP * (i + 4 * s) for s in range(3)), r["lift"][:, i, :].T)
    wl[...] = wf[0:B, 0 : 12 * FP].astype(bf16)
    wf[...] = jnp.zeros_like(wf)
    for i in range(4):
        put3(wf, B * i, (0, 56, 112), r["pproj"][:, i, :])
    wq[...] = wf[0 : 4 * B, 0 : 3 * B].astype(bf16)
    wf[...] = jnp.zeros_like(wf)
    for i in range(4):
        put3(wf, B * i, (0, 56, 112), r["plift"][:, i, :].T)
    wz[...] = wf[0 : 4 * B, 0 : 3 * B].astype(bf16)

    for s, rows, o in lists:
        for ref, offset in ((fr, o), (br, -o)):
            ok, target = inside("dom", -offset)

            @pl.when(jnp.logical_not(ok))
            def _():
                if ref is fr:
                    for k in range(NDER):
                        fr[k, rows] = jnp.zeros((LIST, 128), f32)
                else:
                    br[rows] = jnp.zeros((LIST, 128), f32)

    for s, (axis, o) in enumerate(partners):
        ok, target = inside(axis, -o)

        @pl.when(jnp.logical_not(ok))
        def _():
            hr[s * HALO : (s + 1) * HALO] = jnp.zeros((HALO, 512), f32)

    hr[96:128, :] = jnp.zeros((32, 512), f32)
    br[160:256, :] = jnp.zeros((96, 128), f32)

    loads["cell"].wait()
    for q in range(Q):
        value = cell[q]
        ig[q * B : (q + 1) * B, :] = value
        for half in range(2):
            dh[half][0, q // 2, :, (q % 2) * 128 : (q % 2) * 128 + 128] = value[
                :, half * 128 : half * 128 + 128
            ]
    a[0, 0:B] = cell[0]
    a[0, B : 2 * B] = cell[3] + cell[7]
    a[0, 2 * B :] = cell[3] - cell[7]
    loads["star"].wait()

    def moved(k, half):
        def one(pair):
            width = 256 if pair < 4 else 128
            yh[half][pair, :, 0:width] = dot(w1[...], split_rows(dh[half][k, pair, :, 0:width]))

        return [functools.partial(one, pair) for pair in range(5)]

    def mixed(k, half, weight):
        def one(ct):
            held = {}

            def tile(j, q):
                row = j * B + ct * 8
                lane = (q % 2) * 128
                return yh[half][q // 2, row : row + 8, lane : lane + 128]

            def emit(p, lanes, value):
                rows = slice(ct * 8, ct * 8 + 8)
                lane = (p % 2) * 128
                dh[half][k + 1, p // 2, rows, lane : lane + 128] = value
                at = slice(p * B + ct * 8, p * B + ct * 8 + 8)
                ig[at, lanes] = ig[at, lanes] + value * weight
                if p == 0:
                    a[k + 1, rows, lanes] = value
                if p == 3:
                    held[0] = value
                if p == 7:
                    at = slice(B + ct * 8, B + ct * 8 + 8)
                    a[k + 1, at, lanes] = held[0] + value
                    at = slice(2 * B + ct * 8, 2 * B + ct * 8 + 8)
                    a[k + 1, at, lanes] = held[0] - value

            mix27(star, tile, half, emit)

        return [functools.partial(one, ct) for ct in range(7)]

    def payload(k):
        hi, lo = halves(a[k])
        rows = 2 * B
        fs[k, :, 0:rows] = dot_nt(send_hot, hi[0:rows]) + dot_nt(send_hot, lo[0:rows])
        fs[k, :, rows:] = jnp.zeros((160, 128 - rows), f32)
        gm[k] = dot(hi, minus_hot) + dot(lo, minus_hot)
        fr[k, own_list] = fs[k, own_list]

    def derive(k, weight):
        weight = weight / (k + 2).astype(f32)
        payload(k)
        weave(moved(k, 1), mixed(k, 0, weight))

        @pl.when(k == 3)
        def _():
            pl.semaphore_wait(barrier, count)
            each(fault_moves(0), "start")

        weave(moved(k + 1, 0), mixed(k, 1, weight))
        return weight

    def spread(half):
        lanes = slice(half * 128, half * 128 + 128)

        def one(q):
            vh[half][q] = dot(w2[...], split_rows(ig[q * B : (q + 1) * B, lanes]))

        return [functools.partial(one, q) for q in range(Q)]

    weave(moved(0, 0))
    lax.fori_loop(0, NDER - 2, derive, jnp.float32(1.0))
    last = NDER - 2
    weight = jnp.float32(1.0 / math.factorial(NDER))
    payload(last)
    weave(moved(last, 1), mixed(last, 0, weight))
    weave(spread(0), mixed(last, 1, weight))
    payload(last + 1)
    i_hi, i_lo = halves(ig[...])
    hs[:, 0 : Q * B] = dot_nt(halo_hot, i_hi) + dot_nt(halo_hot, i_lo)
    hs[:, Q * B : 512] = jnp.zeros((96, 512 - Q * B), f32)
    each(fault_moves(1) + halo_moves, "start")
    send_cells = lax.shift_right_arithmetic(send_row, 2)
    shear_hot = jnp.concatenate([onehot(send_cells == iota((N, 256), 0)), minus_hot], axis=1)
    s_hi, s_lo = i_hi[3 * B : 4 * B], i_lo[3 * B : 4 * B]
    face_row = jnp.concatenate([minus_row & 3, plus_row & 3], axis=1)

    def projected(x, row):
        full = dot(wq[...], split_rows(x))
        best = full[3 * B :]
        for i in range(3):
            best = jnp.where(row == i, full[i * B : (i + 1) * B], best)
        return best

    shear = projected(
        dot(s_hi, shear_hot) + dot(s_lo, shear_hot),
        jnp.concatenate([send_row & 3, minus_row & 3], axis=1),
    )
    psi, m_w = shear[:, 0:256], shear[:, 256:]

    loads["fl"].wait()

    def local(half):
        def inner(ct):
            def tile(j, q):
                row = j * B + ct * 8
                return vh[half][q, row : row + 8, :]

            def emit(p, lanes, value):
                rows = slice(ct * 8, ct * 8 + 8)
                u[p, rows, lanes] = cell[p, rows, lanes] + value

            mix27(star, tile, half, emit)

        def face(row):
            mix9(
                fl, row // FP, half, lambda q: vh[half][q, 3 * B + row : 3 * B + row + 8, :], so, row, False
            )

        return [functools.partial(inner, ct) for ct in range(7)] + [
            functools.partial(face, row) for row in range(0, 4 * FP, 8)
        ]

    def table(half):
        for q in range(Q):
            for j in range(4):
                block = vh[half][q, 3 * B + FP * j : 3 * B + FP * (j + 1), :]
                hi = rounded(block)
                town[
                    q * 2 * FP : (q + 1) * 2 * FP, j * N + half * 128 : j * N + half * 128 + 128
                ] = jnp.concatenate([hi, block - hi], axis=0).astype(bf16)

    def arrived(k):
        hi, lo = halves(fr[k])
        gt = (dot(plus_hot, hi) + dot(plus_hot, lo)).T
        for n in range(2):
            both = jnp.concatenate(
                [gm[k, 2 * n * B : 2 * n * B + B], gt[n * B : (n + 1) * B]], axis=1
            )
            best = projected(both, face_row)
            pk[k, n * B : (n + 1) * B] = best[:, 0:SLOTS] + best[:, SLOTS:]

    def near_pick(i):
        hot = masked(onehot(near_col[i : i + 1, :] == iota((N, N), 0)), i)
        pick[i] = dot(town[...], hot)
    weave(local(0), spread(1))
    table(0)
    table(1)
    each(fault_moves(0), "wait_recv")
    weave(local(1), [functools.partial(arrived, k) for k in range(4)] + [functools.partial(near_pick, i) for i in range(4)])

    each(fault_moves(1) + halo_moves, "wait_recv")
    arrived(4)
    arrived(5)
    alive = (iota((1, SLOTS), 1) < r["live"][...]).astype(f32)
    nload, sload, deff = r["nload"][...], r["sload"][...], r["deff"][...]
    factor = 0.5 * jnp.exp(r["svar"][...] / deff)
    total = jnp.zeros((B, SLOTS), f32)
    for t in range(NT):
        normal = pk[0, 0:B]
        tangent = pk[0, B:]
        for k in range(1, NDER):
            normal = normal + POWERS[t][k] * pk[k, 0:B]
            tangent = tangent + POWERS[t][k] * pk[k, B:]
        strength = jnp.maximum(nload - 0.5 * normal, 0.0)
        locked = sload + 0.5 * tangent
        scaled = strength * deff
        curve = scaled * factor
        now = locked / (0.5 + curve)
        for m in range(NEWTON - 1):
            arg = factor * now
            root = jnp.sqrt(1.0 + arg * arg)
            mag = jnp.log(jnp.abs(arg) + root)
            asinh = jnp.where(arg < 0, -mag, mag)
            residue = locked - 0.5 * now - scaled * asinh
            slope = -0.5 - curve / root
            now = now - residue / slope
        sl[t] = (now * alive)[0:NP]
        total = total + MASSES[t] * (locked - sload - 0.5 * now)
    am = (total - m_w) * alive
    ap = jnp.where(iota((B, SLOTS), 0) == NP, alive, total * alive)

    entry_hot = onehot(lax.shift_right_logical(plus_row, 2) == iota((160, SLOTS), 0))
    b_hi, b_lo = halves(jnp.concatenate([ap, jnp.zeros((128 - B, SLOTS), f32)], axis=0))
    bs[...] = dot_nt(entry_hot, b_hi) + dot_nt(entry_hot, b_lo)
    each(back_moves, "start")
    br[own_list, :] = bs[own_list, :]

    ht = hr[...].T
    for q in range(Q):
        full = dot(w2[3 * B :, :], split_rows(ht[q * B : (q + 1) * B, :]))
        for j in range(4):
            block = full[FP * j : FP * (j + 1), :]
            hi = rounded(block)
            thalo[q * 2 * FP : (q + 1) * 2 * FP, j * 128 : (j + 1) * 128] = jnp.concatenate(
                [hi, block - hi], axis=0
            ).astype(bf16)
    loads["fn"].wait()

    def turned(i):
        hot = masked(onehot(near_col[i : i + 1, :] == iota((128, N), 0) + N), i)
        both = pick[i] + dot(thalo[...], hot)
        for q in range(Q):
            hi = both[q * 2 * FP : q * 2 * FP + FP]
            lo = both[q * 2 * FP + FP : (q + 1) * 2 * FP]
            full = dot(wp[...], jnp.concatenate([hi, lo, hi], axis=0).astype(bf16))
            best = full[2 * FP :]
            for h in range(2):
                best = jnp.where(turns[i : i + 1, :] == h, full[h * FP : (h + 1) * FP], best)
            ori[q, i * FP : (i + 1) * FP, :] = best

    def far(i):
        def one(row, half):
            lanes = slice(half * 128, half * 128 + 128)
            mix9(fn, i, half, lambda q: ori[q, row : row + 8, lanes], so, row, True)

        return [
            functools.partial(one, row, half)
            for row in range(i * FP, (i + 1) * FP, 8)
            for half in range(2)
        ]

    weave([functools.partial(turned, 0)])
    for i in range(3):
        weave([functools.partial(turned, i + 1)], far(i))

    am_hi, am_lo = halves(am)

    def own_lift(i):
        own_hot = onehot(wide(minus_col) == iota((SLOTS, N), 1) * 4 + i)
        e_m = dot(am_hi, own_hot) + dot(am_lo, own_hot)
        z[i] = dot(wz[i * B : (i + 1) * B, :], split_rows(e_m))

    def lift(p):
        u[p] = u[p] - dot(wl[...], split_rows(so[p]))

    weave([functools.partial(own_lift, i) for i in range(4)], far(3))
    far_hot = [onehot(wide(send_col) == iota((160, N), 1) * 4 + i) for i in range(4)]
    weave([functools.partial(lift, p) for p in range(Q)])

    each(back_moves, "wait_recv")
    back = br[...].T
    back = back[0:B] - back[NP : NP + 1] * psi
    bt_hi, bt_lo = halves(back[:, 0:160])
    for i in range(4):
        e_p = dot(bt_hi, far_hot[i]) + dot(bt_lo, far_hot[i])
        z_p = dot(wz[i * B : (i + 1) * B, :], split_rows(e_p))
        z_m = z[i]
        z[i] = z_m + z_p
        z[4 + i] = z_m - z_p

    def finish(n, carry):
        at = pl.multiple_of(n * 8, 8)
        rows = pl.ds(at, 8)
        for half in range(2):
            lanes = slice(half * 128, half * 128 + 128)
            tiles = [z[i, rows, lanes] for i in range(8)]
            for p in range(Q):
                acc = u[p, rows, lanes]
                for i in range(4):
                    acc = acc + (
                        fl[p, 3, i : i + 1, lanes] * tiles[i] + fl[p, 7, i : i + 1, lanes] * tiles[4 + i]
                    )
                u[p, rows, lanes] = acc
        return carry

    lax.fori_loop(0, 7, finish, 0)
    each(fault_moves(0) + fault_moves(1) + halo_moves + back_moves, "wait_send")


def per_device(n_group, n_dom, *args):
    args = list(args)
    for at in (1, 4, 5):
        args[at] = args[at].transpose(1, 2, 0, 3)
    for at in (6, 9):
        args[at] = args[at].transpose(1, 0, 2)
    for at in (7, 10):
        args[at] = args[at].transpose(2, 0, 1)
    for at in (15, 17, 19, 20, 21, 22):
        args[at] = args[at].reshape(1, SLOTS)
    return pl.pallas_call(
        functools.partial(kernel, n_group, n_dom),
        out_shape=(pltpu.VMEM((Q, B, N), f32), pltpu.VMEM((NT, NP, SLOTS), f32)),
        in_specs=[pl.BlockSpec(memory_space=pl.ANY)] * len(args),
        out_specs=(pl.BlockSpec(memory_space=pltpu.VMEM),) * 2,
        scratch_shapes=[pltpu.VMEM(x.shape, x.dtype) for x in args] + list(SCRATCH.values()),
        compiler_params=pltpu.CompilerParams(
            collective_id=0, has_side_effects=True, vmem_limit_bytes=56 << 20
        ),
        name="ader_step",
    )(*args)


def solution(mesh):
    both = ("group", "dom")
    return jax.shard_map(
        functools.partial(per_device, mesh.shape["group"], mesh.shape["dom"]),
        mesh=mesh,
        in_specs=(
            P(None, None, both),
            P(None, None, None, both),
            P(),
            P(),
            P(None, None, None, both),
            P(None, None, None, both),
            P(),
            P(),
            P(),
            P(),
            P(),
            P(None, both),
            P(None, both),
            P(both, None),
            P(both, None),
            P(both),
            P(both, None),
            P(both),
            P("group", "dom"),
            P(both),
            P(both),
            P(both),
            P(both),
        ),
        out_specs=(P(None, None, both), P(None, None, both)),
        check_vma=False,
    )
```

```python
import functools
import math

import jax
import jax.numpy as jnp
import numpy as np
from jax import lax
from jax.experimental import pallas as pl
from jax.experimental.pallas import tpu as pltpu
from jax.sharding import PartitionSpec as P

Q = 9
B = 56
FB = 21
FP = 24
NP = 49
NT = 6
NDER = 6
NEWTON = 4
N = 256
SLOTS = 128
LIST = 32
HALO = 16
FROWS = 13 * B
f32 = jnp.float32
bf16 = jnp.bfloat16
i32 = jnp.int32

GAUSS_POINTS = np.array(
    [
        -0.932469514203152,
        -0.6612093864662645,
        -0.2386191860831909,
        0.2386191860831909,
        0.6612093864662645,
        0.932469514203152,
    ]
)
GAUSS_MASSES = np.array(
    [
        0.1713244923791704,
        0.3607615730481386,
        0.467913934572691,
        0.467913934572691,
        0.3607615730481386,
        0.1713244923791704,
    ]
)
NODES = 0.5 * (GAUSS_POINTS + 1.0)
POWERS = [[float(NODES[t] ** k / math.factorial(k)) for k in range(NDER)] for t in range(NT)]
MASSES = [float(0.5 * w) for w in GAUSS_MASSES]
FAULT_OFFSETS = (-2, -1, 0, 1, 2)
NEAR_OFFSETS = (-2, -1, 1, 2)
STRIKE_OFFSETS = (-1, 1)

INPUTS = (
    ["cell", "star", "stiff", "volk", "fl", "fn", "proj", "lift", "perm", "pproj", "plift"]
    + ["neigh", "code", "near", "strike", "fminus", "fsend", "fplus", "live"]
    + ["nload", "sload", "deff", "svar"]
)
SCRATCH = dict(
    d0=pltpu.VMEM((NDER, 5, B, N), f32),
    d1=pltpu.VMEM((NDER, 5, B, N), f32),
    y0=pltpu.VMEM((5, 3 * B, N), f32),
    y1=pltpu.VMEM((5, 3 * B, N), f32),
    v0=pltpu.VMEM((Q, 3 * B + 4 * FP, 128), f32),
    v1=pltpu.VMEM((Q, 3 * B + 4 * FP, 128), f32),
    ig=pltpu.VMEM((Q * B, N), f32),
    so=pltpu.VMEM((Q, 4 * FP, N), f32),
    ori=pltpu.VMEM((Q, 4 * FP, N), f32),
    a=pltpu.VMEM((NDER, 3 * B, N), f32),
    gm=pltpu.VMEM((NDER, 3 * B, SLOTS), f32),
    pk=pltpu.VMEM((NDER, 2 * B, SLOTS), f32),
    town=pltpu.VMEM((Q * 2 * FP, 4 * N), bf16),
    thalo=pltpu.VMEM((Q * 2 * FP, 4 * 128), bf16),
    pick=pltpu.VMEM((4, Q * 2 * FP, N), f32),
    z=pltpu.VMEM((8, B, N), f32),
    hs=pltpu.VMEM((96, 512), f32),
    hr=pltpu.VMEM((128, 512), f32),
    fs=pltpu.VMEM((NDER, 160, 128), f32),
    fr=pltpu.VMEM((NDER, 160, 128), f32),
    bs=pltpu.VMEM((160, 128), f32),
    br=pltpu.VMEM((256, 128), f32),
    wf=pltpu.VMEM((3 * B + 4 * FP, 384), f32),
    w1=pltpu.VMEM((3 * B, 3 * B), bf16),
    w2=pltpu.VMEM((3 * B + 4 * FP, 3 * B), bf16),
    wp=pltpu.VMEM((3 * FP, 3 * FP), bf16),
    wl=pltpu.VMEM((B, 12 * FP), bf16),
    wq=pltpu.VMEM((4 * B, 3 * B), bf16),
    wz=pltpu.VMEM((4 * B, 3 * B), bf16),
    in_sem=pltpu.SemaphoreType.DMA((23,)),
    fault_send_sem=pltpu.SemaphoreType.DMA((2, 4)),
    fault_recv_sem=pltpu.SemaphoreType.DMA((2, 4)),
    send_sem=pltpu.SemaphoreType.DMA((10,)),
    recv_sem=pltpu.SemaphoreType.DMA((10,)),
)


def rounded(x):
    return x.astype(bf16).astype(f32)


def split_rows(x):
    hi = rounded(x)
    return jnp.concatenate([hi, x - hi, hi], axis=0).astype(bf16)


def halves(x):
    hi = x.astype(bf16)
    return hi, (x - hi.astype(f32)).astype(bf16)


def dot(a, b):
    return jnp.dot(a, b, preferred_element_type=f32)


def dot_nt(a, b):
    return lax.dot_general(a, b, (((1,), (1,)), ((), ())), preferred_element_type=f32)


def iota(shape, dim):
    return lax.broadcasted_iota(i32, shape, dim)


def onehot(cond):
    return jnp.where(cond, 1.0, 0.0).astype(bf16)


def column(row):
    return jnp.broadcast_to(row.astype(f32), (128, 128)).T.astype(i32)


def wide(x):
    return jnp.concatenate([x, x], axis=1)


def put3(ref, row, cols, x):
    hi = rounded(x)
    lo = x - hi
    for c, part in zip(cols, (hi, hi, lo)):
        ref[row : row + x.shape[0], c : c + x.shape[1]] = part


def weave(*groups):
    steps = []
    for group in groups:
        steps += [((n + 0.5) / len(group), step) for n, step in enumerate(group)]
    for place, step in sorted(steps, key=lambda item: item[0]):
        step()


def mix27(star, tile, half, emit):
    lanes = slice(half * 128, half * 128 + 128)
    tiles = [[tile(j, q) for q in range(Q)] for j in range(3)]
    for p in range(Q):
        parts = []
        for j in range(3):
            acc = star[p, 0, j : j + 1, lanes] * tiles[j][0]
            for q in range(1, Q):
                acc = acc + star[p, q, j : j + 1, lanes] * tiles[j][q]
            parts.append(acc)
        emit(p, lanes, (parts[0] + parts[1]) + parts[2])


def mix9(flux, i, half, tile, dst, row, add):
    lanes = slice(half * 128, half * 128 + 128)
    tiles = [tile(q) for q in range(Q)]
    for p in range(Q):
        acc = flux[p, 0, i : i + 1, lanes] * tiles[0]
        for q in range(1, Q):
            acc = acc + flux[p, q, i : i + 1, lanes] * tiles[q]
        if add:
            acc = acc + dst[p, row : row + 8, lanes]
        dst[p, row : row + 8, lanes] = acc


def kernel(n_group, n_dom, *refs):
    names = ["u", "sl"] + INPUTS + list(SCRATCH)
    hbm = dict(zip(INPUTS, refs))
    r = dict(zip(names, refs[len(INPUTS) :]))
    cell, star, fl, fn = (r[k] for k in ("cell", "star", "fl", "fn"))
    dh, yh, vh = (r["d0"], r["d1"]), (r["y0"], r["y1"]), (r["v0"], r["v1"])
    ig, u, so, ori, a = (r[k] for k in ("ig", "u", "so", "ori", "a"))
    gm, pk, town, thalo, pick, z = (r[k] for k in ("gm", "pk", "town", "thalo", "pick", "z"))
    hs, hr, fs, fr, bs, br = (r[k] for k in ("hs", "hr", "fs", "fr", "bs", "br"))
    wf, w1, w2, wp, wl, wq, wz = (r[k] for k in ("wf", "w1", "w2", "wp", "wl", "wq", "wz"))
    sl = r["sl"]
    g = lax.axis_index("group")
    me = lax.axis_index("dom")

    large = ["cell", "star", "fl", "fn"]
    order = [name for name in INPUTS if name not in large] + large
    loads = {
        name: pltpu.make_async_copy(hbm[name], r[name], r["in_sem"].at[n])
        for n, name in enumerate(order)
    }
    for name in order:
        loads[name].start()

    def inside(axis, offset):
        at, size = (me, n_dom) if axis == "dom" else (g, n_group)
        target = at + offset
        return jnp.logical_and(target >= 0, target < size), target

    partners = [("dom", o) for o in NEAR_OFFSETS] + [("group", o) for o in STRIKE_OFFSETS]

    barrier = pltpu.get_barrier_semaphore()
    count = 0
    for axis, o in partners:
        ok, target = inside(axis, o)
        count = count + ok.astype(i32)

        @pl.when(ok)
        def _():
            pl.semaphore_signal(
                barrier,
                inc=1,
                device_id={axis: target},
                device_id_type=pl.DeviceIdType.MESH,
            )

    lists = [(s, slice(k * LIST, (k + 1) * LIST), FAULT_OFFSETS[k]) for s, k in enumerate((0, 1, 3, 4))]
    own_list = slice(2 * LIST, 3 * LIST)

    def fault_moves(part):
        orders = (slice(0, 4), slice(4, NDER))[part]
        return [
            (
                fs.at[orders, rows],
                fr.at[orders, rows],
                r["fault_send_sem"].at[part, s],
                r["fault_recv_sem"].at[part, s],
                "dom",
                o,
            )
            for s, rows, o in lists
        ]

    halo_moves = []
    for s, (axis, o) in enumerate(partners):
        rows = slice(s * HALO, (s + 1) * HALO)
        halo_moves.append((hs.at[rows], hr.at[rows], r["send_sem"].at[s], r["recv_sem"].at[s], axis, o))
    back_moves = [
        (bs.at[rows], br.at[rows], r["send_sem"].at[6 + s], r["recv_sem"].at[6 + s], "dom", -o)
        for s, rows, o in lists
    ]

    def each(which, action):
        for axis, o in partners:
            to = -o if action == "wait_recv" else o
            ok, target = inside(axis, to)
            mine = [move for move in which if move[4:] == (axis, o)]
            if not mine:
                continue

            @pl.when(ok)
            def _():
                for src, dst, sent, got, _, _ in mine:
                    copy = pltpu.make_async_remote_copy(
                        src_ref=src,
                        dst_ref=dst,
                        send_sem=sent,
                        recv_sem=got,
                        device_id={axis: target},
                        device_id_type=pl.DeviceIdType.MESH,
                    )
                    getattr(copy, action)()

    for name in order:
        if name not in large:
            loads[name].wait()

    sends = r["fsend"][...]
    send_row = [
        jnp.concatenate([sends[k : k + 1, :] for k in range(4)], axis=1),
        jnp.concatenate([sends[4:5, :], jnp.full((1, 96), -4, i32)], axis=1),
    ]
    send_col = jnp.concatenate([column(row) for row in send_row], axis=0)[0:160]
    send_row = jnp.concatenate(send_row, axis=1)
    near = r["near"][...]
    strike = r["strike"][...]
    halo_row = jnp.concatenate(
        [near[k : k + 1, :] for k in range(4)]
        + [strike[k : k + 1, :] for k in range(2)]
        + [jnp.full((1, 32), -1, i32)],
        axis=1,
    )
    halo_col = column(halo_row)[0:96]
    minus_row = r["fminus"][...]
    minus_col = column(minus_row)
    plus_row = r["fplus"][...]
    plus_col = column(lax.shift_right_logical(plus_row, 2))
    send_hot = onehot(lax.shift_right_arithmetic(wide(send_col), 2) == iota((160, N), 1))
    halo_hot = onehot(wide(halo_col) == iota((96, N), 1))
    minus_hot = onehot(lax.shift_right_logical(minus_row, 2) == iota((N, SLOTS), 0))
    plus_hot = onehot(wide(plus_col)[:, 0:160] == iota((SLOTS, 160), 1))
    codes = r["code"][...]
    faces = (codes >= 3).astype(i32) + (codes >= 6).astype(i32) + (codes >= 9).astype(i32)
    turns = codes - 3 * faces
    near_col = r["neigh"][...]

    def masked(hot, i):
        parts = [
            hot * jnp.broadcast_to(jnp.where(faces[i : i + 1, :] == j, 1.0, 0.0), hot.shape).astype(bf16)
            for j in range(4)
        ]
        return jnp.concatenate(parts, axis=0)


    put3(wf, 0, (0, 56, 112), jnp.concatenate([r["stiff"][j].T for j in range(3)], axis=0))
    w1[...] = wf[0 : 3 * B, 0 : 3 * B].astype(bf16)
    put3(wf, 0, (0, 56, 112), jnp.concatenate([r["volk"][j].T for j in range(3)], axis=0))
    wf[3 * B :, 0 : 3 * B] = jnp.zeros((4 * FP, 3 * B), f32)
    for i in range(4):
        put3(wf, 3 * B + FP * i, (0, 56, 112), r["proj"][:, i, :])
    w2[...] = wf[:, 0 : 3 * B].astype(bf16)
    wf[...] = jnp.zeros_like(wf)
    for h in range(3):
        put3(wf, FP * h, (0, FP, 2 * FP), r["perm"][h])
    wp[...] = wf[0 : 3 * FP, 0 : 3 * FP].astype(bf16)
    wf[...] = jnp.zeros_like(wf)
    for i in range(4):
        put3(wf, 0, tuple(FP * (i + 4 * s) for s in range(3)), r["lift"][:, i, :].T)
    wl[...] = wf[0:B, 0 : 12 * FP].astype(bf16)
    wf[...] = jnp.zeros_like(wf)
    for i in range(4):
        put3(wf, B * i, (0, 56, 112), r["pproj"][:, i, :])
    wq[...] = wf[0 : 4 * B, 0 : 3 * B].astype(bf16)
    wf[...] = jnp.zeros_like(wf)
    for i in range(4):
        put3(wf, B * i, (0, 56, 112), r["plift"][:, i, :].T)
    wz[...] = wf[0 : 4 * B, 0 : 3 * B].astype(bf16)

    for s, rows, o in lists:
        for ref, offset in ((fr, o), (br, -o)):
            ok, target = inside("dom", -offset)

            @pl.when(jnp.logical_not(ok))
            def _():
                if ref is fr:
                    for k in range(NDER):
                        fr[k, rows] = jnp.zeros((LIST, 128), f32)
                else:
                    br[rows] = jnp.zeros((LIST, 128), f32)

    for s, (axis, o) in enumerate(partners):
        ok, target = inside(axis, -o)

        @pl.when(jnp.logical_not(ok))
        def _():
            hr[s * HALO : (s + 1) * HALO] = jnp.zeros((HALO, 512), f32)

    hr[96:128, :] = jnp.zeros((32, 512), f32)
    br[160:256, :] = jnp.zeros((96, 128), f32)

    loads["cell"].wait()
    for q in range(Q):
        value = cell[q]
        ig[q * B : (q + 1) * B, :] = value
        for half in range(2):
            dh[half][0, q // 2, :, (q % 2) * 128 : (q % 2) * 128 + 128] = value[
                :, half * 128 : half * 128 + 128
            ]
    a[0, 0:B] = cell[0]
    a[0, B : 2 * B] = cell[3] + cell[7]
    a[0, 2 * B :] = cell[3] - cell[7]
    loads["star"].wait()

    def moved(k, half):
        def one(pair):
            width = 256 if pair < 4 else 128
            yh[half][pair, :, 0:width] = dot(w1[...], split_rows(dh[half][k, pair, :, 0:width]))

        return [functools.partial(one, pair) for pair in range(5)]

    def mixed(k, half, weight):
        def one(ct):
            held = {}

            def tile(j, q):
                row = j * B + ct * 8
                lane = (q % 2) * 128
                return yh[half][q // 2, row : row + 8, lane : lane + 128]

            def emit(p, lanes, value):
                rows = slice(ct * 8, ct * 8 + 8)
                lane = (p % 2) * 128
                dh[half][k + 1, p // 2, rows, lane : lane + 128] = value
                at = slice(p * B + ct * 8, p * B + ct * 8 + 8)
                ig[at, lanes] = ig[at, lanes] + value * weight
                if p == 0:
                    a[k + 1, rows, lanes] = value
                if p == 3:
                    held[0] = value
                if p == 7:
                    at = slice(B + ct * 8, B + ct * 8 + 8)
                    a[k + 1, at, lanes] = held[0] + value
                    at = slice(2 * B + ct * 8, 2 * B + ct * 8 + 8)
                    a[k + 1, at, lanes] = held[0] - value

            mix27(star, tile, half, emit)

        return [functools.partial(one, ct) for ct in range(7)]

    def payload(k):
        hi, lo = halves(a[k])
        rows = 2 * B
        fs[k, :, 0:rows] = dot_nt(send_hot, hi[0:rows]) + dot_nt(send_hot, lo[0:rows])
        fs[k, :, rows:] = jnp.zeros((160, 128 - rows), f32)
        gm[k] = dot(hi, minus_hot) + dot(lo, minus_hot)
        fr[k, own_list] = fs[k, own_list]

    def derive(k, weight):
        weight = weight / (k + 2).astype(f32)
        payload(k)
        weave(moved(k, 1), mixed(k, 0, weight))

        @pl.when(k == 3)
        def _():
            pl.semaphore_wait(barrier, count)
            each(fault_moves(0), "start")

        weave(moved(k + 1, 0), mixed(k, 1, weight))
        return weight

    def spread(half):
        lanes = slice(half * 128, half * 128 + 128)

        def one(q):
            vh[half][q] = dot(w2[...], split_rows(ig[q * B : (q + 1) * B, lanes]))

        return [functools.partial(one, q) for q in range(Q)]

    weave(moved(0, 0))
    lax.fori_loop(0, NDER - 2, derive, jnp.float32(1.0))
    last = NDER - 2
    weight = jnp.float32(1.0 / math.factorial(NDER))
    payload(last)
    weave(moved(last, 1), mixed(last, 0, weight))
    weave(spread(0), mixed(last, 1, weight))
    payload(last + 1)
    i_hi, i_lo = halves(ig[...])
    hs[:, 0 : Q * B] = dot_nt(halo_hot, i_hi) + dot_nt(halo_hot, i_lo)
    hs[:, Q * B : 512] = jnp.zeros((96, 512 - Q * B), f32)
    each(fault_moves(1) + halo_moves, "start")
    send_cells = lax.shift_right_arithmetic(send_row, 2)
    shear_hot = jnp.concatenate([onehot(send_cells == iota((N, 256), 0)), minus_hot], axis=1)
    s_hi, s_lo = i_hi[3 * B : 4 * B], i_lo[3 * B : 4 * B]
    face_row = jnp.concatenate([minus_row & 3, plus_row & 3], axis=1)

    def projected(x, row):
        full = dot(wq[...], split_rows(x))
        best = full[3 * B :]
        for i in range(3):
            best = jnp.where(row == i, full[i * B : (i + 1) * B], best)
        return best

    shear = projected(
        dot(s_hi, shear_hot) + dot(s_lo, shear_hot),
        jnp.concatenate([send_row & 3, minus_row & 3], axis=1),
    )
    psi, m_w = shear[:, 0:256], shear[:, 256:]

    loads["fl"].wait()

    def local(half):
        def inner(ct):
            def tile(j, q):
                row = j * B + ct * 8
                return vh[half][q, row : row + 8, :]

            def emit(p, lanes, value):
                rows = slice(ct * 8, ct * 8 + 8)
                u[p, rows, lanes] = cell[p, rows, lanes] + value

            mix27(star, tile, half, emit)

        def face(row):
            mix9(
                fl, row // FP, half, lambda q: vh[half][q, 3 * B + row : 3 * B + row + 8, :], so, row, False
            )

        return [functools.partial(inner, ct) for ct in range(7)] + [
            functools.partial(face, row) for row in range(0, 4 * FP, 8)
        ]

    def table(half):
        for q in range(Q):
            for j in range(4):
                block = vh[half][q, 3 * B + FP * j : 3 * B + FP * (j + 1), :]
                hi = rounded(block)
                town[
                    q * 2 * FP : (q + 1) * 2 * FP, j * N + half * 128 : j * N + half * 128 + 128
                ] = jnp.concatenate([hi, block - hi], axis=0).astype(bf16)

    def arrived(k):
        hi, lo = halves(fr[k])
        gt = (dot(plus_hot, hi) + dot(plus_hot, lo)).T
        for n in range(2):
            both = jnp.concatenate(
                [gm[k, 2 * n * B : 2 * n * B + B], gt[n * B : (n + 1) * B]], axis=1
            )
            best = projected(both, face_row)
            pk[k, n * B : (n + 1) * B] = best[:, 0:SLOTS] + best[:, SLOTS:]

    def near_pick(i):
        hot = masked(onehot(near_col[i : i + 1, :] == iota((N, N), 0)), i)
        pick[i] = dot(town[...], hot)
    weave(local(0), spread(1))
    table(0)
    table(1)
    each(fault_moves(0), "wait_recv")
    weave(local(1), [functools.partial(arrived, k) for k in range(4)])

    each(fault_moves(1) + halo_moves, "wait_recv")
    arrived(4)
    arrived(5)
    alive = (iota((1, SLOTS), 1) < r["live"][...]).astype(f32)
    nload, sload, deff = r["nload"][...], r["sload"][...], r["deff"][...]
    factor = 0.5 * jnp.exp(r["svar"][...] / deff)
    total = jnp.zeros((B, SLOTS), f32)
    for t in range(NT):
        normal = pk[0, 0:B]
        tangent = pk[0, B:]
        for k in range(1, NDER):
            normal = normal + POWERS[t][k] * pk[k, 0:B]
            tangent = tangent + POWERS[t][k] * pk[k, B:]
        strength = jnp.maximum(nload - 0.5 * normal, 0.0)
        locked = sload + 0.5 * tangent
        scaled = strength * deff
        curve = scaled * factor
        now = locked / (0.5 + curve)
        for m in range(NEWTON - 1):
            arg = factor * now
            root = jnp.sqrt(1.0 + arg * arg)
            mag = jnp.log(jnp.abs(arg) + root)
            asinh = jnp.where(arg < 0, -mag, mag)
            residue = locked - 0.5 * now - scaled * asinh
            slope = -0.5 - curve / root
            now = now - residue / slope
        sl[t] = (now * alive)[0:NP]
        total = total + MASSES[t] * (locked - sload - 0.5 * now)
    am = (total - m_w) * alive
    ap = jnp.where(iota((B, SLOTS), 0) == NP, alive, total * alive)

    entry_hot = onehot(lax.shift_right_logical(plus_row, 2) == iota((160, SLOTS), 0))
    b_hi, b_lo = halves(jnp.concatenate([ap, jnp.zeros((128 - B, SLOTS), f32)], axis=0))
    bs[...] = dot_nt(entry_hot, b_hi) + dot_nt(entry_hot, b_lo)
    each(back_moves, "start")
    br[own_list, :] = bs[own_list, :]

    weave([functools.partial(near_pick, i) for i in range(4)])
    ht = hr[...].T
    for q in range(Q):
        full = dot(w2[3 * B :, :], split_rows(ht[q * B : (q + 1) * B, :]))
        for j in range(4):
            block = full[FP * j : FP * (j + 1), :]
            hi = rounded(block)
            thalo[q * 2 * FP : (q + 1) * 2 * FP, j * 128 : (j + 1) * 128] = jnp.concatenate(
                [hi, block - hi], axis=0
            ).astype(bf16)
    loads["fn"].wait()

    def turned(i):
        hot = masked(onehot(near_col[i : i + 1, :] == iota((128, N), 0) + N), i)
        both = pick[i] + dot(thalo[...], hot)
        for q in range(Q):
            hi = both[q * 2 * FP : q * 2 * FP + FP]
            lo = both[q * 2 * FP + FP : (q + 1) * 2 * FP]
            full = dot(wp[...], jnp.concatenate([hi, lo, hi], axis=0).astype(bf16))
            best = full[2 * FP :]
            for h in range(2):
                best = jnp.where(turns[i : i + 1, :] == h, full[h * FP : (h + 1) * FP], best)
            ori[q, i * FP : (i + 1) * FP, :] = best

    def far(i):
        def one(row, half):
            lanes = slice(half * 128, half * 128 + 128)
            mix9(fn, i, half, lambda q: ori[q, row : row + 8, lanes], so, row, True)

        return [
            functools.partial(one, row, half)
            for row in range(i * FP, (i + 1) * FP, 8)
            for half in range(2)
        ]

    weave([functools.partial(turned, 0)])
    for i in range(3):
        weave([functools.partial(turned, i + 1)], far(i))

    am_hi, am_lo = halves(am)

    def own_lift(i):
        own_hot = onehot(wide(minus_col) == iota((SLOTS, N), 1) * 4 + i)
        e_m = dot(am_hi, own_hot) + dot(am_lo, own_hot)
        z[i] = dot(wz[i * B : (i + 1) * B, :], split_rows(e_m))

    def lift(p):
        u[p] = u[p] - dot(wl[...], split_rows(so[p]))

    weave([functools.partial(own_lift, i) for i in range(4)], far(3))
    far_hot = [onehot(wide(send_col) == iota((160, N), 1) * 4 + i) for i in range(4)]
    weave([functools.partial(lift, p) for p in range(Q)])

    each(back_moves, "wait_recv")
    back = br[...].T
    back = back[0:B] - back[NP : NP + 1] * psi
    bt_hi, bt_lo = halves(back[:, 0:160])
    for i in range(4):
        e_p = dot(bt_hi, far_hot[i]) + dot(bt_lo, far_hot[i])
        z_p = dot(wz[i * B : (i + 1) * B, :], split_rows(e_p))
        z_m = z[i]
        z[i] = z_m + z_p
        z[4 + i] = z_m - z_p

    def finish(n, carry):
        at = pl.multiple_of(n * 8, 8)
        rows = pl.ds(at, 8)
        for half in range(2):
            lanes = slice(half * 128, half * 128 + 128)
            tiles = [z[i, rows, lanes] for i in range(8)]
            for p in range(Q):
                acc = u[p, rows, lanes]
                for i in range(4):
                    acc = acc + (
                        fl[p, 3, i : i + 1, lanes] * tiles[i] + fl[p, 7, i : i + 1, lanes] * tiles[4 + i]
                    )
                u[p, rows, lanes] = acc
        return carry

    lax.fori_loop(0, 7, finish, 0)
    each(fault_moves(0) + fault_moves(1) + halo_moves + back_moves, "wait_send")


def per_device(n_group, n_dom, *args):
    args = list(args)
    for at in (1, 4, 5):
        args[at] = args[at].transpose(1, 2, 0, 3)
    for at in (6, 9):
        args[at] = args[at].transpose(1, 0, 2)
    for at in (7, 10):
        args[at] = args[at].transpose(2, 0, 1)
    for at in (15, 17, 19, 20, 21, 22):
        args[at] = args[at].reshape(1, SLOTS)
    return pl.pallas_call(
        functools.partial(kernel, n_group, n_dom),
        out_shape=(pltpu.VMEM((Q, B, N), f32), pltpu.VMEM((NT, NP, SLOTS), f32)),
        in_specs=[pl.BlockSpec(memory_space=pl.ANY)] * len(args),
        out_specs=(pl.BlockSpec(memory_space=pltpu.VMEM),) * 2,
        scratch_shapes=[pltpu.VMEM(x.shape, x.dtype) for x in args] + list(SCRATCH.values()),
        compiler_params=pltpu.CompilerParams(
            collective_id=0, has_side_effects=True, vmem_limit_bytes=56 << 20
        ),
        name="ader_step",
    )(*args)


def solution(mesh):
    both = ("group", "dom")
    return jax.shard_map(
        functools.partial(per_device, mesh.shape["group"], mesh.shape["dom"]),
        mesh=mesh,
        in_specs=(
            P(None, None, both),
            P(None, None, None, both),
            P(),
            P(),
            P(None, None, None, both),
            P(None, None, None, both),
            P(),
            P(),
            P(),
            P(),
            P(),
            P(None, both),
            P(None, both),
            P(both, None),
            P(both, None),
            P(both),
            P(both, None),
            P(both),
            P("group", "dom"),
            P(both),
            P(both),
            P(both),
            P(both),
        ),
        out_specs=(P(None, None, both), P(None, None, both)),
        check_vma=False,
    )
```
